32 devices in a mesh: gx: 8 (over z, core), gy: 4 (over y, x).
Axes of the slice: x: 2, y: 2, z: 4, core: 2. Of those that a mesh axis runs over, the one named last changes fastest.
Arguments:
- snapshots: float32 [128, 64, 16, 128], P(None, 'gx', 'gy'), may hold values from -700 to 700
- viscosity: float32 [64, 16, 128], P('gx', 'gy'), may hold values from 0.2 to 1
- velocity: float32 [3, 64, 16, 128], P(None, 'gx', 'gy'), may hold values from -4 to 4
Outputs:
- modes: bfloat16 [128, 64, 16, 128], P(None, 'gx', 'gy')
- factor: float32 [128, 128], replicated
The draws below stay inside these ranges and needn't reach their ends.
All inputs are finite; a program needn't handle non-finite values.
Results may differ from the reference program's by a relative error of at most 0.001.
Values sent between devices are 32-bit elements; how exact they have to be, the bound alone decides.
A program may use at most 64 MiB of HBM per device.

```python
import math
import jax
import jax.numpy as jnp
from jax import lax

SNAPS = 128
CZ = 128
NX = 64
NY = 16


def draw_snapshots(key, part):
    keys = jax.random.split(jax.random.fold_in(key, 7), 5)
    independent = jax.random.truncated_normal(keys[0], -4.0, 4.0, (SNAPS, NX, NY, CZ), jnp.float32)
    common = jax.random.truncated_normal(keys[1], -4.0, 4.0, (NX, NY, CZ), jnp.float32)
    mixing = jax.random.uniform(keys[2], (SNAPS,), jnp.float32, 0.3, 0.9)
    amplitude = jnp.exp(jax.random.uniform(keys[3], (SNAPS,), jnp.float32, 0.0, math.log(10.0)))
    rough = jnp.exp(jax.random.uniform(keys[4], (NX, NY, CZ), jnp.float32, math.log(0.5), math.log(2.0)))
    lagged = jnp.roll(independent, 1, axis=0)
    field = independent + 0.6 * lagged + mixing[:, None, None, None] * common[None]
    return (amplitude[:, None, None, None] * rough[None] * field).astype(jnp.float32)


def steps_of(rng, dims, cuts, low, top_value):
    level, own = 1.0, jax.random.fold_in(rng, 6)
    for dim, blocks in cuts:
        draws = jnp.exp(jax.random.uniform(jax.random.fold_in(own, dim), (blocks,), jnp.float32, low / len(cuts), top_value / len(cuts)))
        level = level * jnp.repeat(draws, dims[dim] // blocks).reshape([-1 if axis == dim else 1 for axis in range(len(dims))])
    return level


def scatter_about(key, extent, scale, limit, pieces=(), kind=jnp.bfloat16):
    values = jax.random.normal(key, extent, jnp.float32) * scale
    if len(pieces) > 0:
        values = steps_of(key, extent, pieces, -0.22, 0.18) * values
    return jnp.clip(values, min=-limit, max=limit).astype(kind)


def setup_inputs(seed: int = 0) -> dict:
    seeds = jax.random.split(jax.random.key(seed), 4)
    snapshots = draw_snapshots(jax.random.fold_in(seeds[3], 71), 0)
    viscosity = jnp.clip(0.2 + 0.8 * jax.random.uniform(seeds[1], (NX, NY, CZ), jnp.float32) ** steps_of(seeds[1], (NX, NY, CZ), ((0, 8), (1, 4)), -0.2, 0.2), 0.2, 1.0)
    velocity = scatter_about(seeds[2], (3, NX, NY, CZ), 1.0, 4.0, ((1, 8), (2, 4)), jnp.float32)
    return {"snapshots": snapshots, "viscosity": viscosity, "velocity": velocity}


def unit_shift(direction, offset):
    shifts = [0, 0, 0]
    shifts[direction] = offset
    return shifts

def take_cells(padded, shifts, sizes):
    return padded[..., 2 + shifts[0]:2 + shifts[0] + sizes[0], 2 + shifts[1]:2 + shifts[1] + sizes[1], 2 + shifts[2]:2 + shifts[2] + sizes[2]]

def stencil(field_pad, visc_pad, velocity):
    sizes = velocity.shape[1:]
    center = take_cells(field_pad, [0, 0, 0], sizes)
    visc_mid = take_cells(visc_pad, [0, 0, 0], sizes)
    total = jnp.zeros(center.shape, jnp.float32)
    for direction in range(3):
        plus_one = take_cells(field_pad, unit_shift(direction, 1), sizes)
        minus_one = take_cells(field_pad, unit_shift(direction, -1), sizes)
        plus_two = take_cells(field_pad, unit_shift(direction, 2), sizes)
        minus_two = take_cells(field_pad, unit_shift(direction, -2), sizes)
        slope = (8.0 * (plus_one - minus_one) - (plus_two - minus_two)) / 12.0
        visc_plus = 0.5 * (visc_mid + take_cells(visc_pad, unit_shift(direction, 1), sizes))
        visc_minus = 0.5 * (visc_mid + take_cells(visc_pad, unit_shift(direction, -1), sizes))
        spread = visc_plus * (plus_one - center) - visc_minus * (center - minus_one)
        total = total + velocity[direction] * slope - spread
    return total

def reference(snapshots, viscosity, velocity):
    visc_pad = jnp.pad(viscosity, 2)

    def one_snapshot(single):
        return stencil(jnp.pad(single, 2), visc_pad, velocity)
    resid = lax.map(one_snapshot, snapshots)
    count_cells = NX * NY * CZ
    matrix = resid.reshape(SNAPS, count_cells)
    gram = jnp.dot(matrix.astype(jnp.float32), matrix.T.astype(jnp.float32), precision=lax.Precision.HIGHEST, preferred_element_type=jnp.float32) / float(count_cells)
    factor = jnp.linalg.cholesky(gram).T
    solved = lax.linalg.triangular_solve(factor, matrix, left_side=True, lower=False, transpose_a=True)
    modes = solved.reshape(SNAPS, NX, NY, CZ).astype(jnp.bfloat16)
    return (modes, factor)
```

```python
import functools

import jax
import jax.numpy as jnp
from jax import lax
from jax.experimental import pallas as pl
from jax.experimental.pallas import tpu as pltpu
from jax.sharding import PartitionSpec as P

MESH = pl.DeviceIdType.MESH
HIGH = lax.Precision.HIGHEST


def dot(a, b, transposed=False):
    return lax.dot_general(
        a, b, (((1,), (1 if transposed else 0,)), ((), ())),
        precision=HIGH, preferred_element_type=jnp.float32,
    )


def kernel(
    dims, peers, chunk, cells_total,
    snap_ref, visc_ref, vel_ref, modes_ref, factor_ref,
    wide, near_visc, pad_visc, coef, resid, rows_out, part_y, part_x, inv, low, diag,
    send_halo, recv_halo, send_visc, recv_visc, send_y, recv_y, send_x, recv_x,
):
    snaps, nx, ny, nz = dims
    gx_n, gy_n = peers
    cells = nx * ny
    chunks = snaps // chunk
    gx, gy = lax.axis_index("gx"), lax.axis_index("gy")

    def along_y(other):
        return {"gx": gx, "gy": other}

    def along_x(other):
        return {"gx": other, "gy": gy}

    barrier = pltpu.get_barrier_semaphore()
    for off in range(1, gy_n):
        pl.semaphore_signal(barrier, inc=1, device_id=along_y(lax.rem(gy + off, gy_n)), device_id_type=MESH)
    for off in range(1, gx_n):
        pl.semaphore_signal(barrier, inc=1, device_id=along_x(lax.rem(gx + off, gx_n)), device_id_type=MESH)

    def spread(p):
        def plane(i, carry):
            for j in range(ny):
                wide[p, i + 2, j + 2] = snap_ref[
                    pl.ds(p * chunk * cells + i * ny + j, chunk, stride=cells), :
                ]
            return carry

        lax.fori_loop(0, nx, plane, 0)

    def halo_copies(p):
        mid_x, mid_y = pl.ds(2, nx), pl.ds(2, ny)
        table = (
            (gy < gy_n - 1, along_y(gy + 1), (mid_x, pl.ds(ny, 2)), (mid_x, pl.ds(0, 2))),
            (gy > 0, along_y(gy - 1), (mid_x, pl.ds(2, 2)), (mid_x, pl.ds(ny + 2, 2))),
            (gx < gx_n - 1, along_x(gx + 1), (pl.ds(nx, 2), mid_y), (pl.ds(0, 2), mid_y)),
            (gx > 0, along_x(gx - 1), (pl.ds(2, 2), mid_y), (pl.ds(nx + 2, 2), mid_y)),
        )
        return [
            (
                there,
                pltpu.make_async_remote_copy(
                    src_ref=wide.at[p, src[0], src[1]],
                    dst_ref=wide.at[p, dst[0], dst[1]],
                    send_sem=send_halo.at[p, way],
                    recv_sem=recv_halo.at[p, way],
                    device_id=who,
                    device_id_type=MESH,
                ),
            )
            for way, (there, who, src, dst) in enumerate(table)
        ]

    def visc_copies():
        table = (
            (gy < gy_n - 1, along_y(gy + 1)),
            (gy > 0, along_y(gy - 1)),
            (gx < gx_n - 1, along_x(gx + 1)),
            (gx > 0, along_x(gx - 1)),
        )
        return [
            (
                there,
                pltpu.make_async_remote_copy(
                    src_ref=visc_ref,
                    dst_ref=near_visc.at[way],
                    send_sem=send_visc.at[way],
                    recv_sem=recv_visc.at[way],
                    device_id=who,
                    device_id_type=MESH,
                ),
            )
            for way, (there, who) in enumerate(table)
        ]

    arrives = (gy > 0, gy < gy_n - 1, gx > 0, gx < gx_n - 1)

    def start(copies):
        for there, copy in copies:
            pl.when(there)(copy.start)

    def wait_recv(copies):
        for way, (_, copy) in enumerate(copies):
            pl.when(arrives[way])(copy.wait_recv)

    def wait_send(copies):
        for there, copy in copies:
            pl.when(there)(copy.wait_send)

    spread(0)
    pl.semaphore_wait(barrier, gx_n + gy_n - 2)
    start(visc_copies())
    start(halo_copies(0))
    for p in range(1, chunks):
        spread(p)
        start(halo_copies(p))

    def border(way):
        rows_y = jnp.zeros((chunks, nx, 2, chunk, nz), jnp.float32)
        rows_x = jnp.zeros((chunks, 2, ny, chunk, nz), jnp.float32)
        if way == 0:
            wide[:, 2:nx + 2, 0:2] = rows_y
        elif way == 1:
            wide[:, 2:nx + 2, ny + 2:ny + 4] = rows_y
        elif way == 2:
            wide[:, 0:2, 2:ny + 2] = rows_x
        else:
            wide[:, nx + 2:nx + 4, 2:ny + 2] = rows_x

    for way in range(4):
        pl.when(jnp.logical_not(arrives[way]))(functools.partial(border, way))

    inv[...] = jnp.zeros_like(inv)
    pad_visc[...] = jnp.zeros_like(pad_visc)
    pad_visc[1:nx + 1, 1:ny + 1, :] = visc_ref[...]
    wait_recv(visc_copies())

    def visc_border(way):
        if way == 0:
            pad_visc[1:nx + 1, 0:1, :] = near_visc[0, :, ny - 1:ny, :]
        elif way == 1:
            pad_visc[1:nx + 1, ny + 1:ny + 2, :] = near_visc[1, :, 0:1, :]
        elif way == 2:
            pad_visc[0:1, 1:ny + 1, :] = near_visc[2, nx - 1:nx, :, :]
        else:
            pad_visc[nx + 1:nx + 2, 1:ny + 1, :] = near_visc[3, 0:1, :, :]

    for way in range(4):
        pl.when(arrives[way])(functools.partial(visc_border, way))

    lane3 = lax.broadcasted_iota(jnp.int32, (nx, ny, nz), 2)
    mid = pad_visc[1:nx + 1, 1:ny + 1, :]
    around = (
        (pad_visc[2:nx + 2, 1:ny + 1, :], pad_visc[0:nx, 1:ny + 1, :]),
        (pad_visc[1:nx + 1, 2:ny + 2, :], pad_visc[1:nx + 1, 0:ny, :]),
        (
            jnp.where(lane3 < nz - 1, pltpu.roll(mid, nz - 1, 2), 0.0),
            jnp.where(lane3 > 0, pltpu.roll(mid, 1, 2), 0.0),
        ),
    )
    for d in range(3):
        coef[d, 0] = vel_ref[d] * (8.0 / 12.0)
        coef[d, 1] = vel_ref[d] * (1.0 / 12.0)
        coef[d, 2] = 0.5 * (mid + around[d][0])
        coef[d, 3] = 0.5 * (mid + around[d][1])

    lane = lax.broadcasted_iota(jnp.int32, (chunk, nz), 1)

    def stencil(p):
        def plane(i, carry):
            for j in range(ny):
                c = wide[p, i + 2, j + 2]
                near = (
                    (wide[p, i + 3, j + 2], wide[p, i + 1, j + 2], wide[p, i + 4, j + 2], wide[p, i, j + 2]),
                    (wide[p, i + 2, j + 3], wide[p, i + 2, j + 1], wide[p, i + 2, j + 4], wide[p, i + 2, j]),
                    (
                        jnp.where(lane < nz - 1, pltpu.roll(c, nz - 1, 1), 0.0),
                        jnp.where(lane > 0, pltpu.roll(c, 1, 1), 0.0),
                        jnp.where(lane < nz - 2, pltpu.roll(c, nz - 2, 1), 0.0),
                        jnp.where(lane > 1, pltpu.roll(c, 2, 1), 0.0),
                    ),
                )
                total = None
                for d in range(3):
                    up, down, up2, down2 = near[d]
                    w8, w1, vp, vm = (coef[d, t, i, pl.ds(j, 1), :] for t in range(4))
                    term = (w8 * (up - down) - w1 * (up2 - down2)) - (vp * (up - c) - vm * (c - down))
                    total = term if total is None else total + term
                resid[pl.ds(p * chunk, chunk), pl.ds(pl.multiple_of((i * ny + j) * nz, nz), nz)] = total
            return carry

        lax.fori_loop(0, nx, plane, 0)

    def sum_copies(p, axis):
        me, count, who, part, send, recv = (
            (gy, gy_n, along_y, part_y, send_y, recv_y) if axis == "gy" else (gx, gx_n, along_x, part_x, send_x, recv_x)
        )
        out, into = [], []
        for off in range(1, count):
            to, frm = lax.rem(me + off, count), lax.rem(me + count - off, count)
            for list_, slot, k in ((out, me, to), (into, frm, frm)):
                list_.append(
                    pltpu.make_async_remote_copy(
                        src_ref=part.at[p, slot], dst_ref=part.at[p, slot],
                        send_sem=send.at[p, off], recv_sem=recv.at[p, off],
                        device_id=who(k), device_id_type=MESH,
                    )
                )
        return out, into

    def added(part, p, count):
        total = part[p, 0]
        for k in range(1, count):
            total = total + part[p, k]
        return total

    def gram(p):
        top = (p + 1) * chunk
        panel = dot(resid[p * chunk:top, :], resid[0:top, :], transposed=True) * (1.0 / cells_total)
        if top < snaps:
            panel = jnp.concatenate([panel, jnp.zeros((chunk, snaps - top), jnp.float32)], axis=1)
        part_y[p, gy] = panel
        for copy in sum_copies(p, "gy")[0]:
            copy.start()

    def gram_x(p):
        for copy in sum_copies(p, "gy")[1]:
            copy.wait_recv()
        part_x[p, gx] = added(part_y, p, gy_n)
        for copy in sum_copies(p, "gx")[0]:
            copy.start()

    row_s = lax.broadcasted_iota(jnp.int32, (chunk, snaps), 0)
    lane_s = lax.broadcasted_iota(jnp.int32, (chunk, snaps), 1)

    def padded(x):
        return x if chunk == snaps else jnp.concatenate([x, jnp.zeros((snaps - chunk, snaps), jnp.float32)], axis=0)

    def factor(p):
        for copy in sum_copies(p, "gx")[1]:
            copy.wait_recv()
        g = added(part_x, p, gx_n)
        w0 = p * chunk
        here = pl.ds(w0, chunk)
        if p > 0:
            off = dot(g, inv[...], transposed=True)
            g = pltpu.roll(g, snaps - w0, 1) - dot(off, padded(off), transposed=True)
            back = dot(off, inv[...])
            low[here, :] = off
        else:
            low[here, :] = jnp.zeros((chunk, snaps), jnp.float32)
        a = jnp.where(lane_s < chunk, g, jnp.where(lane_s == row_s + chunk, 1.0, 0.0))
        for k in range(chunk):
            scaled = a[k:k + 1, :] / a[k:k + 1, k:k + 1]
            a = a - jnp.where(row_s > k, a[:, k:k + 1], 0.0) * scaled
        pivots = jnp.sum(jnp.where(lane_s == row_s, a, 0.0), axis=1, keepdims=True)
        a = a / jnp.sqrt(pivots)
        upper = jnp.where((lane_s >= row_s) & (lane_s < chunk), a, 0.0)
        own = jnp.where(lane_s < chunk, pltpu.roll(a, snaps - chunk, 1), 0.0)
        if p > 0:
            diag[here, :] = pltpu.roll(upper, w0, 1)
            inv[here, :] = pltpu.roll(own, w0, 1) - dot(own, padded(back))
        else:
            diag[here, :] = upper
            inv[here, :] = own

    def modes(p):
        top = (p + 1) * chunk
        weights = inv[p * chunk:top, 0:top]

        def plane(i, carry):
            first = pl.multiple_of(i * ny * nz, ny * nz)
            block = dot(weights, resid[0:top, pl.ds(first, ny * nz)])
            for j in range(ny):
                rows_out[pl.ds(i * ny + j, chunk, stride=cells), :] = block[:, j * nz:(j + 1) * nz]
            return carry

        lax.fori_loop(0, nx, plane, 0)
        modes_ref[p * chunk * cells:top * cells, :] = rows_out[...].astype(jnp.bfloat16)

    for p in range(chunks):
        wait_recv(halo_copies(p))
        stencil(p)
        gram(p)
        if p > 0:
            factor(p - 1)
            modes(p - 1)
        gram_x(p)
    factor(chunks - 1)
    modes(chunks - 1)
    factor_ref[...] = low[...].T + diag[...]

    wait_send(visc_copies())
    for p in range(chunks):
        wait_send(halo_copies(p))
        for axis in ("gy", "gx"):
            for copy in sum_copies(p, axis)[0]:
                copy.wait_send()


def per_device(gx_n, gy_n, snapshots, viscosity, velocity):
    snaps, nx, ny, nz = snapshots.shape
    cells = nx * ny
    chunk = snaps // 4
    chunks = snaps // chunk
    f32 = jnp.float32
    dma = pltpu.SemaphoreType.DMA
    vmem = pl.BlockSpec(memory_space=pltpu.VMEM)
    modes, factor = pl.pallas_call(
        functools.partial(
            kernel, (snaps, nx, ny, nz), (gx_n, gy_n), chunk, float(cells * nz * gx_n * gy_n)
        ),
        out_shape=(
            jax.ShapeDtypeStruct((snaps * cells, nz), jnp.bfloat16),
            jax.ShapeDtypeStruct((snaps, snaps), f32),
        ),
        in_specs=[vmem] * 3,
        out_specs=(vmem, vmem),
        scratch_shapes=[
            pltpu.VMEM((chunks, nx + 4, ny + 4, chunk, nz), f32),
            pltpu.VMEM((4, nx, ny, nz), f32),
            pltpu.VMEM((nx + 2, ny + 2, nz), f32),
            pltpu.VMEM((3, 4, nx, ny, nz), f32),
            pltpu.VMEM((snaps, cells * nz), f32),
            pltpu.VMEM((chunk * cells, nz), f32),
            pltpu.VMEM((chunks, gy_n, chunk, snaps), f32),
            pltpu.VMEM((chunks, gx_n, chunk, snaps), f32),
            pltpu.VMEM((snaps, snaps), f32),
            pltpu.VMEM((snaps, snaps), f32),
            pltpu.VMEM((snaps, snaps), f32),
            dma((chunks, 4)), dma((chunks, 4)), dma((4,)), dma((4,)),
            dma((chunks, gy_n)), dma((chunks, gy_n)), dma((chunks, gx_n)), dma((chunks, gx_n)),
        ],
        compiler_params=pltpu.CompilerParams(
            collective_id=0, has_side_effects=True, vmem_limit_bytes=48 * 1024 * 1024
        ),
        name="pod",
    )(snapshots.reshape(snaps * cells, nz), viscosity, velocity)
    return modes.reshape(snaps, nx, ny, nz), factor


def solution(mesh):
    placed = (P(None, "gx", "gy", None), P("gx", "gy", None), P(None, "gx", "gy", None))
    return jax.shard_map(
        functools.partial(per_device, mesh.shape["gx"], mesh.shape["gy"]),
        mesh=mesh,
        in_specs=placed,
        out_specs=(P(None, "gx", "gy", None), P()),
        check_vma=False,
    )
```

```python
import functools

import jax
import jax.numpy as jnp
from jax import lax
from jax.experimental import pallas as pl
from jax.experimental.pallas import tpu as pltpu
from jax.sharding import PartitionSpec as P

MESH = pl.DeviceIdType.MESH
HIGH = lax.Precision.HIGHEST


def dot(a, b, transposed=False):
    return lax.dot_general(
        a, b, (((1,), (1 if transposed else 0,)), ((), ())),
        precision=HIGH, preferred_element_type=jnp.float32,
    )


def narrow_dot(a, b, transposed=False):
    return lax.dot_general(
        a, b, (((1,), (1 if transposed else 0,)), ((), ())), preferred_element_type=jnp.float32
    )


def kernel(
    dims, peers, chunk, cells_total,
    snap_ref, visc_ref, vel_ref, modes_ref, factor_ref,
    wide, passing, near_visc, pad_visc, coef, high, rest, rows_out, part_y, part_x, inv, low, diag,
    send_halo, recv_halo, send_mid, recv_pass, send_pass, recv_mid, send_visc, recv_visc, send_y, recv_y, send_x, recv_x,
):
    snaps, nx, ny, nz = dims
    gx_n, gy_n = peers
    cells = nx * ny
    chunks = snaps // chunk
    gx, gy = lax.axis_index("gx"), lax.axis_index("gy")

    def along_y(other):
        return {"gx": gx, "gy": other}

    def along_x(other):
        return {"gx": other, "gy": gy}

    barrier = pltpu.get_barrier_semaphore()
    for off in range(1, gy_n):
        pl.semaphore_signal(barrier, inc=1, device_id=along_y(lax.rem(gy + off, gy_n)), device_id_type=MESH)
    for off in range(1, gx_n):
        pl.semaphore_signal(barrier, inc=1, device_id=along_x(lax.rem(gx + off, gx_n)), device_id_type=MESH)

    def spread(p):
        def plane(i, carry):
            for j in range(ny):
                wide[p, i + 2, j + 2] = snap_ref[
                    pl.ds(p * chunk * cells + i * ny + j, chunk, stride=cells), :
                ]
            return carry

        lax.fori_loop(0, nx, plane, 0)

    relayed = gy_n == 4
    if relayed:
        up_direct, down_direct = (gy == 0) | (gy == 2), (gy == 1) | (gy == 3)
        from_below, from_above = down_direct, up_direct
    else:
        up_direct, down_direct = gy < gy_n - 1, gy > 0
        from_below, from_above = gy > 0, gy < gy_n - 1
    half = nx // 2
    halves = (pl.ds(2, half), pl.ds(2 + half, half))
    mids = ((1, ny, 0, 0, (0, 3)), (2, 2, ny + 2, 1, (3, 0)))

    def first_hop(p, slot, h):
        _, row, _, _, relays = mids[slot]
        return pltpu.make_async_remote_copy(
            src_ref=wide.at[p, halves[h], pl.ds(row, 2)], dst_ref=passing.at[p, slot],
            send_sem=send_mid.at[p, int(h)], recv_sem=recv_pass.at[p, slot],
            device_id=along_y(relays[h]), device_id_type=MESH,
        )

    def first_hops(p, me):
        return [first_hop(p, me - 1, h) for h in (1, 0)]

    def second_hop(p, slot, relay):
        source, _, row, _, relays = mids[slot]
        h = relays.index(relay)
        return pltpu.make_async_remote_copy(
            src_ref=passing.at[p, slot], dst_ref=wide.at[p, halves[h], pl.ds(row, 2)],
            send_sem=send_pass.at[p, slot], recv_sem=recv_mid.at[p, h],
            device_id=along_y(3 - source), device_id_type=MESH,
        )

    def when_at(me, body):
        pl.when(gy == me)(body)

    def start_first(p):
        if relayed:
            for me in (1, 2):
                def go(me=me):
                    for copy in first_hops(p, me):
                        copy.start()
                when_at(me, go)

    def pass_on(p, late):
        if relayed:
            for relay in (0, 3):
                def go(relay=relay):
                    slot = (relay == 3) ^ (not late)
                    copy = second_hop(p, int(slot), relay)
                    first_hop(p, int(slot), mids[slot][4].index(relay)).wait_recv()
                    copy.start()
                when_at(relay, go)

    def wait_mid(p):
        if relayed:
            for me in (1, 2):
                def go(me=me):
                    for relay in mids[2 - me][4]:
                        second_hop(p, 2 - me, relay).wait_recv()
                when_at(me, go)

    def wait_mid_sent(p):
        if relayed:
            for me in (1, 2):
                def go(me=me):
                    for copy in first_hops(p, me):
                        copy.wait_send()
                when_at(me, go)

    def wait_passed(p):
        if relayed:
            for relay in (0, 3):
                def go(relay=relay):
                    for slot in range(2):
                        second_hop(p, slot, relay).wait_send()
                when_at(relay, go)

    def halo_copies(p):
        mid_x, mid_y = pl.ds(2, nx), pl.ds(2, ny)
        table = (
            (up_direct, along_y(gy + 1), (mid_x, pl.ds(ny, 2)), (mid_x, pl.ds(0, 2))),
            (down_direct, along_y(gy - 1), (mid_x, pl.ds(2, 2)), (mid_x, pl.ds(ny + 2, 2))),
            (gx < gx_n - 1, along_x(gx + 1), (pl.ds(nx, 2), mid_y), (pl.ds(0, 2), mid_y)),
            (gx > 0, along_x(gx - 1), (pl.ds(2, 2), mid_y), (pl.ds(nx + 2, 2), mid_y)),
        )
        return [
            (
                there,
                pltpu.make_async_remote_copy(
                    src_ref=wide.at[p, src[0], src[1]],
                    dst_ref=wide.at[p, dst[0], dst[1]],
                    send_sem=send_halo.at[p, way],
                    recv_sem=recv_halo.at[p, way],
                    device_id=who,
                    device_id_type=MESH,
                ),
            )
            for way, (there, who, src, dst) in enumerate(table)
        ]

    def visc_copies():
        table = (
            (gy < gy_n - 1, along_y(gy + 1)),
            (gy > 0, along_y(gy - 1)),
            (gx < gx_n - 1, along_x(gx + 1)),
            (gx > 0, along_x(gx - 1)),
        )
        return [
            (
                there,
                pltpu.make_async_remote_copy(
                    src_ref=visc_ref,
                    dst_ref=near_visc.at[way],
                    send_sem=send_visc.at[way],
                    recv_sem=recv_visc.at[way],
                    device_id=who,
                    device_id_type=MESH,
                ),
            )
            for way, (there, who) in enumerate(table)
        ]

    arrives = (gy > 0, gy < gy_n - 1, gx > 0, gx < gx_n - 1)
    arrives_direct = (from_below, from_above) + arrives[2:]

    def start(copies):
        for there, copy in copies:
            pl.when(there)(copy.start)

    def wait_recv(copies, comes):
        for way, (_, copy) in enumerate(copies):
            pl.when(comes[way])(copy.wait_recv)

    def wait_send(copies):
        for there, copy in copies:
            pl.when(there)(copy.wait_send)

    spread(0)
    pl.semaphore_wait(barrier, gx_n + gy_n - 2)
    start(visc_copies())

    def send_chunk(p):
        start_first(p)
        start(halo_copies(p))

    send_chunk(0)
    for p in range(1, chunks):
        spread(p)
        if p == 1:
            send_chunk(1)

    def border(way):
        rows_y = jnp.zeros((chunks, nx, 2, chunk, nz), jnp.float32)
        rows_x = jnp.zeros((chunks, 2, ny, chunk, nz), jnp.float32)
        if way == 0:
            wide[:, 2:nx + 2, 0:2] = rows_y
        elif way == 1:
            wide[:, 2:nx + 2, ny + 2:ny + 4] = rows_y
        elif way == 2:
            wide[:, 0:2, 2:ny + 2] = rows_x
        else:
            wide[:, nx + 2:nx + 4, 2:ny + 2] = rows_x

    for way in range(4):
        pl.when(jnp.logical_not(arrives[way]))(functools.partial(border, way))

    inv[...] = jnp.zeros_like(inv)
    pad_visc[...] = jnp.zeros_like(pad_visc)
    pad_visc[1:nx + 1, 1:ny + 1, :] = visc_ref[...]
    wait_recv(visc_copies(), arrives)

    def visc_border(way):
        if way == 0:
            pad_visc[1:nx + 1, 0:1, :] = near_visc[0, :, ny - 1:ny, :]
        elif way == 1:
            pad_visc[1:nx + 1, ny + 1:ny + 2, :] = near_visc[1, :, 0:1, :]
        elif way == 2:
            pad_visc[0:1, 1:ny + 1, :] = near_visc[2, nx - 1:nx, :, :]
        else:
            pad_visc[nx + 1:nx + 2, 1:ny + 1, :] = near_visc[3, 0:1, :, :]

    for way in range(4):
        pl.when(arrives[way])(functools.partial(visc_border, way))

    lane3 = lax.broadcasted_iota(jnp.int32, (nx, ny, nz), 2)
    mid = pad_visc[1:nx + 1, 1:ny + 1, :]
    around = (
        (pad_visc[2:nx + 2, 1:ny + 1, :], pad_visc[0:nx, 1:ny + 1, :]),
        (pad_visc[1:nx + 1, 2:ny + 2, :], pad_visc[1:nx + 1, 0:ny, :]),
        (
            jnp.where(lane3 < nz - 1, pltpu.roll(mid, nz - 1, 2), 0.0),
            jnp.where(lane3 > 0, pltpu.roll(mid, 1, 2), 0.0),
        ),
    )
    for d in range(3):
        coef[d, 0] = vel_ref[d] * (8.0 / 12.0)
        coef[d, 1] = vel_ref[d] * (1.0 / 12.0)
        coef[d, 2] = 0.5 * (mid + around[d][0])
        coef[d, 3] = 0.5 * (mid + around[d][1])

    lane = lax.broadcasted_iota(jnp.int32, (chunk, nz), 1)

    def stencil(p):
        def plane(i, carry):
            for j in range(ny):
                c = wide[p, i + 2, j + 2]
                near = (
                    (wide[p, i + 3, j + 2], wide[p, i + 1, j + 2], wide[p, i + 4, j + 2], wide[p, i, j + 2]),
                    (wide[p, i + 2, j + 3], wide[p, i + 2, j + 1], wide[p, i + 2, j + 4], wide[p, i + 2, j]),
                    (
                        jnp.where(lane < nz - 1, pltpu.roll(c, nz - 1, 1), 0.0),
                        jnp.where(lane > 0, pltpu.roll(c, 1, 1), 0.0),
                        jnp.where(lane < nz - 2, pltpu.roll(c, nz - 2, 1), 0.0),
                        jnp.where(lane > 1, pltpu.roll(c, 2, 1), 0.0),
                    ),
                )
                total = None
                for d in range(3):
                    up, down, up2, down2 = near[d]
                    w8, w1, vp, vm = (coef[d, t, i, pl.ds(j, 1), :] for t in range(4))
                    term = (w8 * (up - down) - w1 * (up2 - down2)) - (vp * (up - c) - vm * (c - down))
                    total = term if total is None else total + term
                lanes = pl.ds(pl.multiple_of((i * ny + j) * nz, nz), nz)
                upper = total.astype(jnp.bfloat16)
                high[pl.ds(p * chunk, chunk), lanes] = upper
                rest[pl.ds(p * chunk, chunk), lanes] = (total - upper.astype(jnp.float32)).astype(jnp.bfloat16)
            return carry

        lax.fori_loop(0, nx, plane, 0)

    def sum_copies(p, axis):
        me, count, who, part, send, recv = (
            (gy, gy_n, along_y, part_y, send_y, recv_y) if axis == "gy" else (gx, gx_n, along_x, part_x, send_x, recv_x)
        )
        out, into = [], []
        for off in range(1, count):
            to, frm = lax.rem(me + off, count), lax.rem(me + count - off, count)
            for list_, slot, k in ((out, me, to), (into, frm, frm)):
                list_.append(
                    pltpu.make_async_remote_copy(
                        src_ref=part.at[p, slot], dst_ref=part.at[p, slot],
                        send_sem=send.at[p, off], recv_sem=recv.at[p, off],
                        device_id=who(k), device_id_type=MESH,
                    )
                )
        return out, into

    def added(part, p, count):
        total = part[p, 0]
        for k in range(1, count):
            total = total + part[p, k]
        return total

    def halves_sum(with_high, with_rest):
        return with_high[:chunk] + (with_high[chunk:] + (with_rest[:chunk] + with_rest[chunk:]))

    def gram(p):
        top = (p + 1) * chunk
        both = jnp.concatenate([high[p * chunk:top, :], rest[p * chunk:top, :]], axis=0)
        panel = halves_sum(narrow_dot(both, high[0:top, :], True), narrow_dot(both, rest[0:top, :], True))
        panel = panel * (1.0 / cells_total)
        if top < snaps:
            panel = jnp.concatenate([panel, jnp.zeros((chunk, snaps - top), jnp.float32)], axis=1)
        part_y[p, gy] = panel
        for copy in sum_copies(p, "gy")[0]:
            copy.start()

    def gram_x(p):
        for copy in sum_copies(p, "gy")[1]:
            copy.wait_recv()
        part_x[p, gx] = added(part_y, p, gy_n)
        for copy in sum_copies(p, "gx")[0]:
            copy.start()

    row_s = lax.broadcasted_iota(jnp.int32, (chunk, snaps), 0)
    lane_s = lax.broadcasted_iota(jnp.int32, (chunk, snaps), 1)

    def padded(x):
        return x if chunk == snaps else jnp.concatenate([x, jnp.zeros((snaps - chunk, snaps), jnp.float32)], axis=0)

    def factor(p):
        for copy in sum_copies(p, "gx")[1]:
            copy.wait_recv()
        g = added(part_x, p, gx_n)
        w0 = p * chunk
        here = pl.ds(w0, chunk)
        if p > 0:
            off = dot(g, inv[...], transposed=True)
            g = pltpu.roll(g, snaps - w0, 1) - dot(off, padded(off), transposed=True)
            back = dot(off, inv[...])
            low[here, :] = off
        else:
            low[here, :] = jnp.zeros((chunk, snaps), jnp.float32)
        a = jnp.where(lane_s < chunk, g, jnp.where(lane_s == row_s + chunk, 1.0, 0.0))
        step = 8
        for first in range(0, chunk, step):
            columns = [jnp.broadcast_to(a[:, first + t:first + t + 1], a.shape) for t in range(step)]
            rows = [a[first + t:first + t + 1, :] for t in range(step)]
            for t in range(step):
                k = first + t
                col = columns[t]
                over = 1.0 / col[k:k + 1, :]
                scaled = rows[t] * over
                a = a - jnp.where(row_s > k, col, 0.0) * scaled
                for u in range(t + 1, step):
                    entry = col[first + u:first + u + 1, :]
                    columns[u] = columns[u] - col * (entry * over)
                    rows[u] = rows[u] - entry * scaled
        pivots = jnp.sum(jnp.where(lane_s == row_s, a, 0.0), axis=1, keepdims=True)
        a = a / jnp.sqrt(pivots)
        upper = jnp.where((lane_s >= row_s) & (lane_s < chunk), a, 0.0)
        own = jnp.where(lane_s < chunk, pltpu.roll(a, snaps - chunk, 1), 0.0)
        if p > 0:
            diag[here, :] = pltpu.roll(upper, w0, 1)
            inv[here, :] = pltpu.roll(own, w0, 1) - dot(own, padded(back))
        else:
            diag[here, :] = upper
            inv[here, :] = own

    def modes(p):
        top = (p + 1) * chunk
        full = inv[p * chunk:top, 0:top]
        upper = full.astype(jnp.bfloat16)
        weights = jnp.concatenate([upper, (full - upper.astype(jnp.float32)).astype(jnp.bfloat16)], axis=0)

        def plane(i, carry):
            first = pl.multiple_of(i * ny * nz, ny * nz)
            lanes = pl.ds(first, ny * nz)
            block = halves_sum(narrow_dot(weights, high[0:top, lanes]), narrow_dot(weights, rest[0:top, lanes]))
            for j in range(ny):
                rows_out[pl.ds(i * ny + j, chunk, stride=cells), :] = block[:, j * nz:(j + 1) * nz]
            return carry

        lax.fori_loop(0, nx, plane, 0)
        modes_ref[p * chunk * cells:top * cells, :] = rows_out[...].astype(jnp.bfloat16)

    for p in range(chunks):
        if p == 0:
            pass_on(0, False)
            pass_on(0, True)
            pass_on(1, False)
        wait_recv(halo_copies(p), arrives_direct)
        wait_mid(p)
        if p + 2 < chunks:
            wait_send(halo_copies(p))
            wait_mid_sent(p)
            send_chunk(p + 2)
        stencil(p)
        gram(p)
        if p + 1 < chunks:
            pass_on(p + 1, True)
        if p > 0:
            factor(p - 1)
        gram_x(p)
        if p + 2 < chunks:
            pass_on(p + 2, False)
        if p > 0:
            modes(p - 1)
    factor(chunks - 1)
    modes(chunks - 1)
    factor_ref[...] = low[...].T + diag[...]

    wait_send(visc_copies())
    for p in range(chunks):
        if p + 2 >= chunks:
            wait_send(halo_copies(p))
            wait_mid_sent(p)
        wait_passed(p)
        for axis in ("gy", "gx"):
            for copy in sum_copies(p, axis)[0]:
                copy.wait_send()


def per_device(gx_n, gy_n, snapshots, viscosity, velocity):
    snaps, nx, ny, nz = snapshots.shape
    cells = nx * ny
    chunk = snaps // 4
    chunks = snaps // chunk
    f32 = jnp.float32
    dma = pltpu.SemaphoreType.DMA
    vmem = pl.BlockSpec(memory_space=pltpu.VMEM)
    modes, factor = pl.pallas_call(
        functools.partial(
            kernel, (snaps, nx, ny, nz), (gx_n, gy_n), chunk, float(cells * nz * gx_n * gy_n)
        ),
        out_shape=(
            jax.ShapeDtypeStruct((snaps * cells, nz), jnp.bfloat16),
            jax.ShapeDtypeStruct((snaps, snaps), f32),
        ),
        in_specs=[vmem] * 3,
        out_specs=(vmem, vmem),
        scratch_shapes=[
            pltpu.VMEM((chunks, nx + 4, ny + 4, chunk, nz), f32),
            pltpu.VMEM((chunks, 2, nx // 2, 2, chunk, nz), f32),
            pltpu.VMEM((4, nx, ny, nz), f32),
            pltpu.VMEM((nx + 2, ny + 2, nz), f32),
            pltpu.VMEM((3, 4, nx, ny, nz), f32),
            pltpu.VMEM((snaps, cells * nz), jnp.bfloat16),
            pltpu.VMEM((snaps, cells * nz), jnp.bfloat16),
            pltpu.VMEM((chunk * cells, nz), f32),
            pltpu.VMEM((chunks, gy_n, chunk, snaps), f32),
            pltpu.VMEM((chunks, gx_n, chunk, snaps), f32),
            pltpu.VMEM((snaps, snaps), f32),
            pltpu.VMEM((snaps, snaps), f32),
            pltpu.VMEM((snaps, snaps), f32),
            dma((chunks, 4)), dma((chunks, 4)), dma((chunks, 2)), dma((chunks, 2)), dma((chunks, 2)), dma((chunks, 2)),
            dma((4,)), dma((4,)),
            dma((chunks, gy_n)), dma((chunks, gy_n)), dma((chunks, gx_n)), dma((chunks, gx_n)),
        ],
        compiler_params=pltpu.CompilerParams(
            collective_id=0, has_side_effects=True, vmem_limit_bytes=48 * 1024 * 1024
        ),
        name="pod",
    )(snapshots.reshape(snaps * cells, nz), viscosity, velocity)
    return modes.reshape(snaps, nx, ny, nz), factor


def solution(mesh):
    placed = (P(None, "gx", "gy", None), P("gx", "gy", None), P(None, "gx", "gy", None))
    return jax.shard_map(
        functools.partial(per_device, mesh.shape["gx"], mesh.shape["gy"]),
        mesh=mesh,
        in_specs=placed,
        out_specs=(P(None, "gx", "gy", None), P()),
        check_vma=False,
    )
```

```python
import functools

import jax
import jax.numpy as jnp
from jax import lax
from jax.experimental import pallas as pl
from jax.experimental.pallas import tpu as pltpu
from jax.sharding import PartitionSpec as P

MESH = pl.DeviceIdType.MESH
HIGH = lax.Precision.HIGHEST


def dot(a, b, transposed=False):
    return lax.dot_general(
        a, b, (((1,), (1 if transposed else 0,)), ((), ())),
        precision=HIGH, preferred_element_type=jnp.float32,
    )


def narrow_dot(a, b, transposed=False):
    return lax.dot_general(
        a, b, (((1,), (1 if transposed else 0,)), ((), ())), preferred_element_type=jnp.float32
    )


def kernel(
    dims, peers, chunk, cells_total,
    snap_any, visc_any, vel_any, modes_ref, factor_ref,
    snap_ref, visc_ref, vel_ref, load_snap, load_rest, wide, passing, near_visc, pad_visc, coef, high, rest, rows_out, part_y, part_x, inv, low, diag,
    send_halo, recv_halo, send_mid, recv_pass, send_pass, recv_mid, send_visc, recv_visc, send_y, recv_y, send_x, recv_x,
):
    snaps, nx, ny, nz = dims
    gx_n, gy_n = peers
    cells = nx * ny
    chunks = snaps // chunk
    gx, gy = lax.axis_index("gx"), lax.axis_index("gy")

    def along_y(other):
        return {"gx": gx, "gy": other}

    def along_x(other):
        return {"gx": other, "gy": gy}

    def load(p):
        here = pl.ds(p * chunk * cells, chunk * cells)
        return pltpu.make_async_copy(snap_any.at[here], snap_ref.at[here], load_snap.at[p])

    load_visc = pltpu.make_async_copy(visc_any, visc_ref, load_rest.at[0])
    load_vel = pltpu.make_async_copy(vel_any, vel_ref, load_rest.at[1])
    load(0).start()
    load_visc.start()
    for p in range(1, chunks):
        load(p).start()
    load_vel.start()

    barrier = pltpu.get_barrier_semaphore()
    for off in range(1, gy_n):
        pl.semaphore_signal(barrier, inc=1, device_id=along_y(lax.rem(gy + off, gy_n)), device_id_type=MESH)
    for off in range(1, gx_n):
        pl.semaphore_signal(barrier, inc=1, device_id=along_x(lax.rem(gx + off, gx_n)), device_id_type=MESH)

    def spread(p):
        def plane(i, carry):
            for j in range(ny):
                wide[p, i + 2, j + 2] = snap_ref[
                    pl.ds(p * chunk * cells + i * ny + j, chunk, stride=cells), :
                ]
            return carry

        lax.fori_loop(0, nx, plane, 0)

    relayed = gy_n == 4
    if relayed:
        up_direct, down_direct = (gy == 0) | (gy == 2), (gy == 1) | (gy == 3)
        from_below, from_above = down_direct, up_direct
    else:
        up_direct, down_direct = gy < gy_n - 1, gy > 0
        from_below, from_above = gy > 0, gy < gy_n - 1
    half = nx // 2
    halves = (pl.ds(2, half), pl.ds(2 + half, half))
    mids = ((1, ny, 0, 0, (0, 3)), (2, 2, ny + 2, 1, (3, 0)))

    def first_hop(p, slot, h):
        _, row, _, _, relays = mids[slot]
        return pltpu.make_async_remote_copy(
            src_ref=wide.at[p, halves[h], pl.ds(row, 2)], dst_ref=passing.at[p, slot],
            send_sem=send_mid.at[p, int(h)], recv_sem=recv_pass.at[p, slot],
            device_id=along_y(relays[h]), device_id_type=MESH,
        )

    def first_hops(p, me):
        return [first_hop(p, me - 1, h) for h in (1, 0)]

    def second_hop(p, slot, relay):
        source, _, row, _, relays = mids[slot]
        h = relays.index(relay)
        return pltpu.make_async_remote_copy(
            src_ref=passing.at[p, slot], dst_ref=wide.at[p, halves[h], pl.ds(row, 2)],
            send_sem=send_pass.at[p, slot], recv_sem=recv_mid.at[p, h],
            device_id=along_y(3 - source), device_id_type=MESH,
        )

    def when_at(me, body):
        pl.when(gy == me)(body)

    def start_first(p):
        if relayed:
            for me in (1, 2):
                def go(me=me):
                    for copy in first_hops(p, me):
                        copy.start()
                when_at(me, go)

    def pass_on(p, late):
        if relayed:
            for relay in (0, 3):
                def go(relay=relay):
                    slot = (relay == 3) ^ (not late)
                    copy = second_hop(p, int(slot), relay)
                    first_hop(p, int(slot), mids[slot][4].index(relay)).wait_recv()
                    copy.start()
                when_at(relay, go)

    def wait_mid(p):
        if relayed:
            for me in (1, 2):
                def go(me=me):
                    for relay in mids[2 - me][4]:
                        second_hop(p, 2 - me, relay).wait_recv()
                when_at(me, go)

    def wait_mid_sent(p):
        if relayed:
            for me in (1, 2):
                def go(me=me):
                    for copy in first_hops(p, me):
                        copy.wait_send()
                when_at(me, go)

    def wait_passed(p):
        if relayed:
            for relay in (0, 3):
                def go(relay=relay):
                    for slot in range(2):
                        second_hop(p, slot, relay).wait_send()
                when_at(relay, go)

    def halo_copies(p):
        mid_x, mid_y = pl.ds(2, nx), pl.ds(2, ny)
        table = (
            (up_direct, along_y(gy + 1), (mid_x, pl.ds(ny, 2)), (mid_x, pl.ds(0, 2))),
            (down_direct, along_y(gy - 1), (mid_x, pl.ds(2, 2)), (mid_x, pl.ds(ny + 2, 2))),
            (gx < gx_n - 1, along_x(gx + 1), (pl.ds(nx, 2), mid_y), (pl.ds(0, 2), mid_y)),
            (gx > 0, along_x(gx - 1), (pl.ds(2, 2), mid_y), (pl.ds(nx + 2, 2), mid_y)),
        )
        return [
            (
                there,
                pltpu.make_async_remote_copy(
                    src_ref=wide.at[p, src[0], src[1]],
                    dst_ref=wide.at[p, dst[0], dst[1]],
                    send_sem=send_halo.at[p, way],
                    recv_sem=recv_halo.at[p, way],
                    device_id=who,
                    device_id_type=MESH,
                ),
            )
            for way, (there, who, src, dst) in enumerate(table)
        ]

    def visc_copies():
        table = (
            (gy < gy_n - 1, along_y(gy + 1)),
            (gy > 0, along_y(gy - 1)),
            (gx < gx_n - 1, along_x(gx + 1)),
            (gx > 0, along_x(gx - 1)),
        )
        return [
            (
                there,
                pltpu.make_async_remote_copy(
                    src_ref=visc_ref,
                    dst_ref=near_visc.at[way],
                    send_sem=send_visc.at[way],
                    recv_sem=recv_visc.at[way],
                    device_id=who,
                    device_id_type=MESH,
                ),
            )
            for way, (there, who) in enumerate(table)
        ]

    arrives = (gy > 0, gy < gy_n - 1, gx > 0, gx < gx_n - 1)
    arrives_direct = (from_below, from_above) + arrives[2:]

    def start(copies):
        for there, copy in copies:
            pl.when(there)(copy.start)

    def wait_recv(copies, comes):
        for way, (_, copy) in enumerate(copies):
            pl.when(comes[way])(copy.wait_recv)

    def wait_send(copies):
        for there, copy in copies:
            pl.when(there)(copy.wait_send)

    load(0).wait()
    spread(0)
    load_visc.wait()
    pl.semaphore_wait(barrier, gx_n + gy_n - 2)

    def send_chunk(p):
        start_first(p)
        start(halo_copies(p))

    send_chunk(0)
    start(visc_copies())
    for p in range(1, chunks):
        load(p).wait()
        spread(p)
        if p == 1:
            send_chunk(1)
    load_vel.wait()

    def border(way):
        rows_y = jnp.zeros((chunks, nx, 2, chunk, nz), jnp.float32)
        rows_x = jnp.zeros((chunks, 2, ny, chunk, nz), jnp.float32)
        if way == 0:
            wide[:, 2:nx + 2, 0:2] = rows_y
        elif way == 1:
            wide[:, 2:nx + 2, ny + 2:ny + 4] = rows_y
        elif way == 2:
            wide[:, 0:2, 2:ny + 2] = rows_x
        else:
            wide[:, nx + 2:nx + 4, 2:ny + 2] = rows_x

    for way in range(4):
        pl.when(jnp.logical_not(arrives[way]))(functools.partial(border, way))

    inv[...] = jnp.zeros_like(inv)
    pad_visc[...] = jnp.zeros_like(pad_visc)
    pad_visc[1:nx + 1, 1:ny + 1, :] = visc_ref[...]
    wait_recv(visc_copies(), arrives)

    def visc_border(way):
        if way == 0:
            pad_visc[1:nx + 1, 0:1, :] = near_visc[0, :, ny - 1:ny, :]
        elif way == 1:
            pad_visc[1:nx + 1, ny + 1:ny + 2, :] = near_visc[1, :, 0:1, :]
        elif way == 2:
            pad_visc[0:1, 1:ny + 1, :] = near_visc[2, nx - 1:nx, :, :]
        else:
            pad_visc[nx + 1:nx + 2, 1:ny + 1, :] = near_visc[3, 0:1, :, :]

    for way in range(4):
        pl.when(arrives[way])(functools.partial(visc_border, way))

    lane3 = lax.broadcasted_iota(jnp.int32, (nx, ny, nz), 2)
    mid = pad_visc[1:nx + 1, 1:ny + 1, :]
    around = (
        (pad_visc[2:nx + 2, 1:ny + 1, :], pad_visc[0:nx, 1:ny + 1, :]),
        (pad_visc[1:nx + 1, 2:ny + 2, :], pad_visc[1:nx + 1, 0:ny, :]),
        (
            jnp.where(lane3 < nz - 1, pltpu.roll(mid, nz - 1, 2), 0.0),
            jnp.where(lane3 > 0, pltpu.roll(mid, 1, 2), 0.0),
        ),
    )
    for d in range(3):
        coef[d, 0] = vel_ref[d] * (8.0 / 12.0)
        coef[d, 1] = vel_ref[d] * (1.0 / 12.0)
        coef[d, 2] = 0.5 * (mid + around[d][0])
        coef[d, 3] = 0.5 * (mid + around[d][1])

    lane = lax.broadcasted_iota(jnp.int32, (chunk, nz), 1)

    def stencil(p):
        def plane(i, carry):
            for j in range(ny):
                c = wide[p, i + 2, j + 2]
                near = (
                    (wide[p, i + 3, j + 2], wide[p, i + 1, j + 2], wide[p, i + 4, j + 2], wide[p, i, j + 2]),
                    (wide[p, i + 2, j + 3], wide[p, i + 2, j + 1], wide[p, i + 2, j + 4], wide[p, i + 2, j]),
                    (
                        jnp.where(lane < nz - 1, pltpu.roll(c, nz - 1, 1), 0.0),
                        jnp.where(lane > 0, pltpu.roll(c, 1, 1), 0.0),
                        jnp.where(lane < nz - 2, pltpu.roll(c, nz - 2, 1), 0.0),
                        jnp.where(lane > 1, pltpu.roll(c, 2, 1), 0.0),
                    ),
                )
                total = None
                for d in range(3):
                    up, down, up2, down2 = near[d]
                    w8, w1, vp, vm = (coef[d, t, i, pl.ds(j, 1), :] for t in range(4))
                    term = (w8 * (up - down) - w1 * (up2 - down2)) - (vp * (up - c) - vm * (c - down))
                    total = term if total is None else total + term
                lanes = pl.ds(pl.multiple_of((i * ny + j) * nz, nz), nz)
                upper = total.astype(jnp.bfloat16)
                high[pl.ds(p * chunk, chunk), lanes] = upper
                rest[pl.ds(p * chunk, chunk), lanes] = (total - upper.astype(jnp.float32)).astype(jnp.bfloat16)
            return carry

        lax.fori_loop(0, nx, plane, 0)

    def sum_copies(p, axis):
        me, count, who, part, send, recv = (
            (gy, gy_n, along_y, part_y, send_y, recv_y) if axis == "gy" else (gx, gx_n, along_x, part_x, send_x, recv_x)
        )
        out, into = [], []
        for off in range(1, count):
            to, frm = lax.rem(me + off, count), lax.rem(me + count - off, count)
            for list_, slot, k in ((out, me, to), (into, frm, frm)):
                list_.append(
                    pltpu.make_async_remote_copy(
                        src_ref=part.at[p, slot], dst_ref=part.at[p, slot],
                        send_sem=send.at[p, off], recv_sem=recv.at[p, off],
                        device_id=who(k), device_id_type=MESH,
                    )
                )
        return out, into

    def added(part, p, count):
        total = part[p, 0]
        for k in range(1, count):
            total = total + part[p, k]
        return total

    def halves_sum(with_high, with_rest):
        return with_high[:chunk] + (with_high[chunk:] + (with_rest[:chunk] + with_rest[chunk:]))

    def gram(p):
        top = (p + 1) * chunk
        both = jnp.concatenate([high[p * chunk:top, :], rest[p * chunk:top, :]], axis=0)
        panel = halves_sum(narrow_dot(both, high[0:top, :], True), narrow_dot(both, rest[0:top, :], True))
        panel = panel * (1.0 / cells_total)
        if top < snaps:
            panel = jnp.concatenate([panel, jnp.zeros((chunk, snaps - top), jnp.float32)], axis=1)
        part_y[p, gy] = panel
        for copy in sum_copies(p, "gy")[0]:
            copy.start()

    def gram_x(p):
        for copy in sum_copies(p, "gy")[1]:
            copy.wait_recv()
        part_x[p, gx] = added(part_y, p, gy_n)
        for copy in sum_copies(p, "gx")[0]:
            copy.start()

    row_s = lax.broadcasted_iota(jnp.int32, (chunk, snaps), 0)
    lane_s = lax.broadcasted_iota(jnp.int32, (chunk, snaps), 1)

    def padded(x):
        return x if chunk == snaps else jnp.concatenate([x, jnp.zeros((snaps - chunk, snaps), jnp.float32)], axis=0)

    def factor(p):
        for copy in sum_copies(p, "gx")[1]:
            copy.wait_recv()
        g = added(part_x, p, gx_n)
        w0 = p * chunk
        here = pl.ds(w0, chunk)
        if p > 0:
            off = dot(g, inv[...], transposed=True)
            g = pltpu.roll(g, snaps - w0, 1) - dot(off, padded(off), transposed=True)
            back = dot(off, inv[...])
            low[here, :] = off
        else:
            low[here, :] = jnp.zeros((chunk, snaps), jnp.float32)
        a = jnp.where(lane_s < chunk, g, jnp.where(lane_s == row_s + chunk, 1.0, 0.0))
        step = 8
        a = a.reshape(chunk // step, step, snaps)
        row_8 = lax.broadcasted_iota(jnp.int32, (step, snaps), 0)

        def splat(x, row):
            return jnp.broadcast_to(x[row:row + 1, :], (step, snaps))

        done = []
        for block in range(chunk // step):
            first = block * step
            own_rows, later = a[0], a[1:]
            columns = [jnp.broadcast_to(later[:, :, first + t:first + t + 1], later.shape) for t in range(step)]
            own_cols = [jnp.broadcast_to(own_rows[:, first + t:first + t + 1], (step, snaps)) for t in range(step)]
            entries = {(t, u): splat(own_cols[t], u) for t in range(step) for u in range(t, step)}
            rows = [splat(own_rows, t) for t in range(step)]
            for t in range(step):
                over = 1.0 / entries[t, t]
                scaled = rows[t] * over
                if later.shape[0]:
                    later = later - columns[t] * scaled[None]
                for u in range(t + 1, step):
                    ratio = entries[t, u] * over
                    for v in range(u, step):
                        entries[u, v] = entries[u, v] - ratio * entries[t, v]
                    rows[u] = rows[u] - ratio * rows[t]
                    if later.shape[0]:
                        columns[u] = columns[u] - columns[t] * ratio[None]
            kept = rows[0]
            for t in range(1, step):
                kept = jnp.where(row_8 == t, rows[t], kept)
            done.append(kept)
            a = later
        a = jnp.concatenate(done, axis=0)
        pivots = jnp.sum(jnp.where(lane_s == row_s, a, 0.0), axis=1, keepdims=True)
        a = a / jnp.sqrt(pivots)
        upper = jnp.where((lane_s >= row_s) & (lane_s < chunk), a, 0.0)
        own = jnp.where(lane_s < chunk, pltpu.roll(a, snaps - chunk, 1), 0.0)
        if p > 0:
            diag[here, :] = pltpu.roll(upper, w0, 1)
            inv[here, :] = pltpu.roll(own, w0, 1) - dot(own, padded(back))
        else:
            diag[here, :] = upper
            inv[here, :] = own

    def modes(p):
        top = (p + 1) * chunk
        full = inv[p * chunk:top, 0:top]
        upper = full.astype(jnp.bfloat16)
        weights = jnp.concatenate([upper, (full - upper.astype(jnp.float32)).astype(jnp.bfloat16)], axis=0)

        def plane(i, carry):
            first = pl.multiple_of(i * ny * nz, ny * nz)
            lanes = pl.ds(first, ny * nz)
            block = halves_sum(narrow_dot(weights, high[0:top, lanes]), narrow_dot(weights, rest[0:top, lanes]))
            for j in range(ny):
                rows_out[pl.ds(i * ny + j, chunk, stride=cells), :] = block[:, j * nz:(j + 1) * nz]
            return carry

        lax.fori_loop(0, nx, plane, 0)
        modes_ref[p * chunk * cells:top * cells, :] = rows_out[...].astype(jnp.bfloat16)

    for p in range(chunks):
        if p == 0:
            pass_on(0, False)
            pass_on(0, True)
            pass_on(1, False)
        wait_recv(halo_copies(p), arrives_direct)
        wait_mid(p)
        if p + 2 < chunks:
            wait_send(halo_copies(p))
            wait_mid_sent(p)
            send_chunk(p + 2)
        stencil(p)
        gram(p)
        if p + 1 < chunks:
            pass_on(p + 1, True)
        if p > 0:
            factor(p - 1)
        gram_x(p)
        if p + 2 < chunks:
            pass_on(p + 2, False)
        if p > 0:
            modes(p - 1)
    factor(chunks - 1)
    modes(chunks - 1)
    factor_ref[...] = low[...].T + diag[...]

    wait_send(visc_copies())
    for p in range(chunks):
        if p + 2 >= chunks:
            wait_send(halo_copies(p))
            wait_mid_sent(p)
        wait_passed(p)
        for axis in ("gy", "gx"):
            for copy in sum_copies(p, axis)[0]:
                copy.wait_send()


def per_device(gx_n, gy_n, snapshots, viscosity, velocity):
    snaps, nx, ny, nz = snapshots.shape
    cells = nx * ny
    chunk = snaps // 4
    chunks = snaps // chunk
    f32 = jnp.float32
    dma = pltpu.SemaphoreType.DMA
    vmem = pl.BlockSpec(memory_space=pltpu.VMEM)
    modes, factor = pl.pallas_call(
        functools.partial(
            kernel, (snaps, nx, ny, nz), (gx_n, gy_n), chunk, float(cells * nz * gx_n * gy_n)
        ),
        out_shape=(
            jax.ShapeDtypeStruct((snaps * cells, nz), jnp.bfloat16),
            jax.ShapeDtypeStruct((snaps, snaps), f32),
        ),
        in_specs=[pl.BlockSpec(memory_space=pl.ANY)] * 3,
        out_specs=(vmem, vmem),
        scratch_shapes=[
            pltpu.VMEM((snaps * cells, nz), f32),
            pltpu.VMEM((nx, ny, nz), f32),
            pltpu.VMEM((3, nx, ny, nz), f32),
            dma((chunks,)), dma((2,)),
            pltpu.VMEM((chunks, nx + 4, ny + 4, chunk, nz), f32),
            pltpu.VMEM((chunks, 2, nx // 2, 2, chunk, nz), f32),
            pltpu.VMEM((4, nx, ny, nz), f32),
            pltpu.VMEM((nx + 2, ny + 2, nz), f32),
            pltpu.VMEM((3, 4, nx, ny, nz), f32),
            pltpu.VMEM((snaps, cells * nz), jnp.bfloat16),
            pltpu.VMEM((snaps, cells * nz), jnp.bfloat16),
            pltpu.VMEM((chunk * cells, nz), f32),
            pltpu.VMEM((chunks, gy_n, chunk, snaps), f32),
            pltpu.VMEM((chunks, gx_n, chunk, snaps), f32),
            pltpu.VMEM((snaps, snaps), f32),
            pltpu.VMEM((snaps, snaps), f32),
            pltpu.VMEM((snaps, snaps), f32),
            dma((chunks, 4)), dma((chunks, 4)), dma((chunks, 2)), dma((chunks, 2)), dma((chunks, 2)), dma((chunks, 2)),
            dma((4,)), dma((4,)),
            dma((chunks, gy_n)), dma((chunks, gy_n)), dma((chunks, gx_n)), dma((chunks, gx_n)),
        ],
        compiler_params=pltpu.CompilerParams(
            collective_id=0, has_side_effects=True, vmem_limit_bytes=60 * 1024 * 1024
        ),
        name="pod",
    )(snapshots.reshape(snaps * cells, nz), viscosity, velocity)
    return modes.reshape(snaps, nx, ny, nz), factor


def solution(mesh):
    placed = (P(None, "gx", "gy", None), P("gx", "gy", None), P(None, "gx", "gy", None))
    return jax.shard_map(
        functools.partial(per_device, mesh.shape["gx"], mesh.shape["gy"]),
        mesh=mesh,
        in_specs=placed,
        out_specs=(P(None, "gx", "gy", None), P()),
        check_vma=False,
    )
```

```python
import functools

import jax
import jax.numpy as jnp
from jax import lax
from jax.experimental import pallas as pl
from jax.experimental.pallas import tpu as pltpu
from jax.sharding import PartitionSpec as P

MESH = pl.DeviceIdType.MESH
HIGH = lax.Precision.HIGHEST


def dot(a, b, transposed=False):
    return lax.dot_general(
        a, b, (((1,), (1 if transposed else 0,)), ((), ())),
        precision=HIGH, preferred_element_type=jnp.float32,
    )


def narrow_dot(a, b, transposed=False):
    return lax.dot_general(
        a, b, (((1,), (1 if transposed else 0,)), ((), ())), preferred_element_type=jnp.float32
    )


def kernel(
    dims, peers, chunk, cells_total,
    snap_any, visc_any, vel_any, modes_ref, factor_ref,
    snap_ref, visc_ref, vel_ref, load_snap, load_rest, wide, passing, near_visc, pad_visc, coef, high, rest, rows_out, part_y, part_x, inv, low, diag,
    send_halo, recv_halo, send_mid, recv_pass, send_pass, recv_mid, send_visc, recv_visc, send_y, recv_y, send_x, recv_x,
):
    snaps, nx, ny, nz = dims
    gx_n, gy_n = peers
    cells = nx * ny
    chunks = snaps // chunk
    gx, gy = lax.axis_index("gx"), lax.axis_index("gy")

    def along_y(other):
        return {"gx": gx, "gy": other}

    def along_x(other):
        return {"gx": other, "gy": gy}

    def load(p):
        here = pl.ds(p * chunk * cells, chunk * cells)
        return pltpu.make_async_copy(snap_any.at[here], snap_ref.at[here], load_snap.at[p])

    load_visc = pltpu.make_async_copy(visc_any, visc_ref, load_rest.at[0])
    load_vel = pltpu.make_async_copy(vel_any, vel_ref, load_rest.at[1])
    load(0).start()
    load_visc.start()
    for p in range(1, chunks):
        load(p).start()
    load_vel.start()

    barrier = pltpu.get_barrier_semaphore()
    for off in range(1, gy_n):
        pl.semaphore_signal(barrier, inc=1, device_id=along_y(lax.rem(gy + off, gy_n)), device_id_type=MESH)
    for off in range(1, gx_n):
        pl.semaphore_signal(barrier, inc=1, device_id=along_x(lax.rem(gx + off, gx_n)), device_id_type=MESH)

    def spread(p):
        def plane(i, carry):
            for j in range(ny):
                wide[p, i + 2, j + 2] = snap_ref[
                    pl.ds(p * chunk * cells + i * ny + j, chunk, stride=cells), :
                ]
            return carry

        lax.fori_loop(0, nx, plane, 0)

    relayed = gy_n == 4
    if relayed:
        up_direct, down_direct = (gy == 0) | (gy == 2), (gy == 1) | (gy == 3)
        from_below, from_above = down_direct, up_direct
    else:
        up_direct, down_direct = gy < gy_n - 1, gy > 0
        from_below, from_above = gy > 0, gy < gy_n - 1
    half = nx // 2
    halves = (pl.ds(2, half), pl.ds(2 + half, half))
    mids = ((1, ny, 0, 0, (0, 3)), (2, 2, ny + 2, 1, (3, 0)))

    def first_hop(p, slot, h):
        _, row, _, _, relays = mids[slot]
        return pltpu.make_async_remote_copy(
            src_ref=wide.at[p, halves[h], pl.ds(row, 2)], dst_ref=passing.at[p, slot],
            send_sem=send_mid.at[p, int(h)], recv_sem=recv_pass.at[p, slot],
            device_id=along_y(relays[h]), device_id_type=MESH,
        )

    def first_hops(p, me):
        return [first_hop(p, me - 1, h) for h in (1, 0)]

    def second_hop(p, slot, relay):
        source, _, row, _, relays = mids[slot]
        h = relays.index(relay)
        return pltpu.make_async_remote_copy(
            src_ref=passing.at[p, slot], dst_ref=wide.at[p, halves[h], pl.ds(row, 2)],
            send_sem=send_pass.at[p, slot], recv_sem=recv_mid.at[p, h],
            device_id=along_y(3 - source), device_id_type=MESH,
        )

    def when_at(me, body):
        pl.when(gy == me)(body)

    def start_first(p):
        if relayed:
            for me in (1, 2):
                def go(me=me):
                    for copy in first_hops(p, me):
                        copy.start()
                when_at(me, go)

    def pass_on(p, late):
        if relayed:
            for relay in (0, 3):
                def go(relay=relay):
                    slot = (relay == 3) ^ (not late)
                    copy = second_hop(p, int(slot), relay)
                    first_hop(p, int(slot), mids[slot][4].index(relay)).wait_recv()
                    copy.start()
                when_at(relay, go)

    def wait_mid(p):
        if relayed:
            for me in (1, 2):
                def go(me=me):
                    for relay in mids[2 - me][4]:
                        second_hop(p, 2 - me, relay).wait_recv()
                when_at(me, go)

    def wait_mid_sent(p):
        if relayed:
            for me in (1, 2):
                def go(me=me):
                    for copy in first_hops(p, me):
                        copy.wait_send()
                when_at(me, go)

    def wait_passed(p):
        if relayed:
            for relay in (0, 3):
                def go(relay=relay):
                    for slot in range(2):
                        second_hop(p, slot, relay).wait_send()
                when_at(relay, go)

    def halo_copies(p):
        mid_x, mid_y = pl.ds(2, nx), pl.ds(2, ny)
        table = (
            (up_direct, along_y(gy + 1), (mid_x, pl.ds(ny, 2)), (mid_x, pl.ds(0, 2))),
            (down_direct, along_y(gy - 1), (mid_x, pl.ds(2, 2)), (mid_x, pl.ds(ny + 2, 2))),
            (gx < gx_n - 1, along_x(gx + 1), (pl.ds(nx, 2), mid_y), (pl.ds(0, 2), mid_y)),
            (gx > 0, along_x(gx - 1), (pl.ds(2, 2), mid_y), (pl.ds(nx + 2, 2), mid_y)),
        )
        return [
            (
                there,
                pltpu.make_async_remote_copy(
                    src_ref=wide.at[p, src[0], src[1]],
                    dst_ref=wide.at[p, dst[0], dst[1]],
                    send_sem=send_halo.at[p, way],
                    recv_sem=recv_halo.at[p, way],
                    device_id=who,
                    device_id_type=MESH,
                ),
            )
            for way, (there, who, src, dst) in enumerate(table)
        ]

    def visc_copies():
        table = (
            (gy < gy_n - 1, along_y(gy + 1)),
            (gy > 0, along_y(gy - 1)),
            (gx < gx_n - 1, along_x(gx + 1)),
            (gx > 0, along_x(gx - 1)),
        )
        return [
            (
                there,
                pltpu.make_async_remote_copy(
                    src_ref=visc_ref,
                    dst_ref=near_visc.at[way],
                    send_sem=send_visc.at[way],
                    recv_sem=recv_visc.at[way],
                    device_id=who,
                    device_id_type=MESH,
                ),
            )
            for way, (there, who) in enumerate(table)
        ]

    arrives = (gy > 0, gy < gy_n - 1, gx > 0, gx < gx_n - 1)
    arrives_direct = (from_below, from_above) + arrives[2:]

    def start(copies):
        for there, copy in copies:
            pl.when(there)(copy.start)

    def wait_recv(copies, comes):
        for way, (_, copy) in enumerate(copies):
            pl.when(comes[way])(copy.wait_recv)

    def wait_send(copies):
        for there, copy in copies:
            pl.when(there)(copy.wait_send)

    load(0).wait()
    spread(0)
    load_visc.wait()
    pl.semaphore_wait(barrier, gx_n + gy_n - 2)

    def send_chunk(p):
        start_first(p)
        start(halo_copies(p))

    send_chunk(0)
    start(visc_copies())
    for p in range(1, chunks):
        load(p).wait()
        spread(p)
        if p == 1:
            send_chunk(1)
    load_vel.wait()

    def border(way):
        rows_y = jnp.zeros((chunks, nx, 2, chunk, nz), jnp.float32)
        rows_x = jnp.zeros((chunks, 2, ny, chunk, nz), jnp.float32)
        if way == 0:
            wide[:, 2:nx + 2, 0:2] = rows_y
        elif way == 1:
            wide[:, 2:nx + 2, ny + 2:ny + 4] = rows_y
        elif way == 2:
            wide[:, 0:2, 2:ny + 2] = rows_x
        else:
            wide[:, nx + 2:nx + 4, 2:ny + 2] = rows_x

    for way in range(4):
        pl.when(jnp.logical_not(arrives[way]))(functools.partial(border, way))

    inv[...] = jnp.zeros_like(inv)
    pad_visc[...] = jnp.zeros_like(pad_visc)
    pad_visc[1:nx + 1, 1:ny + 1, :] = visc_ref[...]
    wait_recv(visc_copies(), arrives)

    def visc_border(way):
        if way == 0:
            pad_visc[1:nx + 1, 0:1, :] = near_visc[0, :, ny - 1:ny, :]
        elif way == 1:
            pad_visc[1:nx + 1, ny + 1:ny + 2, :] = near_visc[1, :, 0:1, :]
        elif way == 2:
            pad_visc[0:1, 1:ny + 1, :] = near_visc[2, nx - 1:nx, :, :]
        else:
            pad_visc[nx + 1:nx + 2, 1:ny + 1, :] = near_visc[3, 0:1, :, :]

    for way in range(4):
        pl.when(arrives[way])(functools.partial(visc_border, way))

    lane3 = lax.broadcasted_iota(jnp.int32, (nx, ny, nz), 2)
    mid = pad_visc[1:nx + 1, 1:ny + 1, :]
    around = (
        (pad_visc[2:nx + 2, 1:ny + 1, :], pad_visc[0:nx, 1:ny + 1, :]),
        (pad_visc[1:nx + 1, 2:ny + 2, :], pad_visc[1:nx + 1, 0:ny, :]),
        (
            jnp.where(lane3 < nz - 1, pltpu.roll(mid, nz - 1, 2), 0.0),
            jnp.where(lane3 > 0, pltpu.roll(mid, 1, 2), 0.0),
        ),
    )
    for d in range(3):
        coef[d, 0] = vel_ref[d] * (8.0 / 12.0)
        coef[d, 1] = vel_ref[d] * (1.0 / 12.0)
        coef[d, 2] = 0.5 * (mid + around[d][0])
        coef[d, 3] = 0.5 * (mid + around[d][1])

    lane = lax.broadcasted_iota(jnp.int32, (chunk, nz), 1)

    def stencil(p):
        def plane(i, carry):
            for j in range(ny):
                c = wide[p, i + 2, j + 2]
                near = (
                    (wide[p, i + 3, j + 2], wide[p, i + 1, j + 2], wide[p, i + 4, j + 2], wide[p, i, j + 2]),
                    (wide[p, i + 2, j + 3], wide[p, i + 2, j + 1], wide[p, i + 2, j + 4], wide[p, i + 2, j]),
                    (
                        jnp.where(lane < nz - 1, pltpu.roll(c, nz - 1, 1), 0.0),
                        jnp.where(lane > 0, pltpu.roll(c, 1, 1), 0.0),
                        jnp.where(lane < nz - 2, pltpu.roll(c, nz - 2, 1), 0.0),
                        jnp.where(lane > 1, pltpu.roll(c, 2, 1), 0.0),
                    ),
                )
                total = None
                for d in range(3):
                    up, down, up2, down2 = near[d]
                    w8, w1, vp, vm = (coef[d, t, i, pl.ds(j, 1), :] for t in range(4))
                    term = (w8 * (up - down) - w1 * (up2 - down2)) - (vp * (up - c) - vm * (c - down))
                    total = term if total is None else total + term
                lanes = pl.ds(pl.multiple_of((i * ny + j) * nz, nz), nz)
                upper = total.astype(jnp.bfloat16)
                high[pl.ds(p * chunk, chunk), lanes] = upper
                rest[pl.ds(p * chunk, chunk), lanes] = (total - upper.astype(jnp.float32)).astype(jnp.bfloat16)
            return carry

        lax.fori_loop(0, nx, plane, 0)

    def sum_copies(p, axis):
        me, count, who, part, send, recv = (
            (gy, gy_n, along_y, part_y, send_y, recv_y) if axis == "gy" else (gx, gx_n, along_x, part_x, send_x, recv_x)
        )
        out, into = [], []
        for off in range(1, count):
            to, frm = lax.rem(me + off, count), lax.rem(me + count - off, count)
            for list_, slot, k in ((out, me, to), (into, frm, frm)):
                list_.append(
                    pltpu.make_async_remote_copy(
                        src_ref=part.at[p, slot], dst_ref=part.at[p, slot],
                        send_sem=send.at[p, off], recv_sem=recv.at[p, off],
                        device_id=who(k), device_id_type=MESH,
                    )
                )
        return out, into

    def added(part, p, count):
        total = part[p, 0]
        for k in range(1, count):
            total = total + part[p, k]
        return total

    def halves_sum(with_high, with_rest):
        return with_high[:chunk] + (with_high[chunk:] + (with_rest[:chunk] + with_rest[chunk:]))

    def gram(p):
        top = (p + 1) * chunk
        both = jnp.concatenate([high[p * chunk:top, :], rest[p * chunk:top, :]], axis=0)
        panel = halves_sum(narrow_dot(both, high[0:top, :], True), narrow_dot(both, rest[0:top, :], True))
        panel = panel * (1.0 / cells_total)
        if top < snaps:
            panel = jnp.concatenate([panel, jnp.zeros((chunk, snaps - top), jnp.float32)], axis=1)
        part_y[p, gy] = panel
        for copy in sum_copies(p, "gy")[0]:
            copy.start()

    def gram_x(p):
        for copy in sum_copies(p, "gy")[1]:
            copy.wait_recv()
        part_x[p, gx] = added(part_y, p, gy_n)
        for copy in sum_copies(p, "gx")[0]:
            copy.start()

    row_s = lax.broadcasted_iota(jnp.int32, (chunk, snaps), 0)
    lane_s = lax.broadcasted_iota(jnp.int32, (chunk, snaps), 1)

    def padded(x):
        return x if chunk == snaps else jnp.concatenate([x, jnp.zeros((snaps - chunk, snaps), jnp.float32)], axis=0)

    def factor(p):
        for copy in sum_copies(p, "gx")[1]:
            copy.wait_recv()
        g = added(part_x, p, gx_n)
        w0 = p * chunk
        here = pl.ds(w0, chunk)
        if p > 0:
            off = dot(g, inv[...], transposed=True)
            g = pltpu.roll(g, snaps - w0, 1) - dot(off, padded(off), transposed=True)
            back = dot(off, inv[...])
            low[here, :] = off
        else:
            low[here, :] = jnp.zeros((chunk, snaps), jnp.float32)
        a = jnp.where(lane_s < chunk, g, jnp.where(lane_s == row_s + chunk, 1.0, 0.0))
        step = 8
        a = a.reshape(chunk // step, step, snaps)
        row_8 = lax.broadcasted_iota(jnp.int32, (step, snaps), 0)

        def splat(x, row):
            return jnp.broadcast_to(x[row:row + 1, :], (step, snaps))

        done = []
        for block in range(chunk // step):
            first = block * step
            own_rows, later = a[0], a[1:]
            columns = [jnp.broadcast_to(later[:, :, first + t:first + t + 1], later.shape) for t in range(step)]
            own_cols = [jnp.broadcast_to(own_rows[:, first + t:first + t + 1], (step, snaps)) for t in range(step)]
            entries = {(t, u): splat(own_cols[t], u) for t in range(step) for u in range(t, step)}
            rows = [splat(own_rows, t) for t in range(step)]
            for t in range(step):
                over = 1.0 / entries[t, t]
                scaled = rows[t] * over
                if later.shape[0]:
                    later = later - columns[t] * scaled[None]
                for u in range(t + 1, step):
                    ratio = entries[t, u] * over
                    for v in range(u, step):
                        entries[u, v] = entries[u, v] - ratio * entries[t, v]
                    rows[u] = rows[u] - ratio * rows[t]
                    if later.shape[0]:
                        columns[u] = columns[u] - columns[t] * ratio[None]
            kept = rows[0]
            for t in range(1, step):
                kept = jnp.where(row_8 == t, rows[t], kept)
            done.append(kept)
            a = later
        a = jnp.concatenate(done, axis=0)
        pivots = jnp.sum(jnp.where(lane_s == row_s, a, 0.0), axis=1, keepdims=True)
        a = a / jnp.sqrt(pivots)
        upper = jnp.where((lane_s >= row_s) & (lane_s < chunk), a, 0.0)
        own = jnp.where(lane_s < chunk, pltpu.roll(a, snaps - chunk, 1), 0.0)
        if p > 0:
            diag[here, :] = pltpu.roll(upper, w0, 1)
            inv[here, :] = pltpu.roll(own, w0, 1) - dot(own, padded(back))
        else:
            diag[here, :] = upper
            inv[here, :] = own

    def modes(p):
        top = (p + 1) * chunk
        full = inv[p * chunk:top, 0:top]
        upper = full.astype(jnp.bfloat16)
        weights = jnp.concatenate([upper, (full - upper.astype(jnp.float32)).astype(jnp.bfloat16)], axis=0)

        def plane(i, carry):
            first = pl.multiple_of(i * ny * nz, ny * nz)
            lanes = pl.ds(first, ny * nz)
            block = halves_sum(narrow_dot(weights, high[0:top, lanes]), narrow_dot(weights, rest[0:top, lanes]))
            for j in range(ny):
                rows_out[pl.ds(i * ny + j, chunk, stride=cells), :] = block[:, j * nz:(j + 1) * nz]
            return carry

        lax.fori_loop(0, nx, plane, 0)
        modes_ref[p * chunk * cells:top * cells, :] = rows_out[...].astype(jnp.bfloat16)

    for p in range(chunks):
        if p == 0:
            pass_on(0, False)
            pass_on(0, True)
            pass_on(1, False)
        wait_recv(halo_copies(p), arrives_direct)
        wait_mid(p)
        if p + 2 < chunks:
            wait_send(halo_copies(p))
            wait_mid_sent(p)
            send_chunk(p + 2)
        stencil(p)
        gram(p)
        if p > 0:
            factor(p - 1)
        gram_x(p)
        if p + 2 < chunks:
            pass_on(p + 2, False)
        if p > 0:
            modes(p - 1)
        if p + 1 < chunks:
            pass_on(p + 1, True)
    factor(chunks - 1)
    modes(chunks - 1)
    factor_ref[...] = low[...].T + diag[...]

    wait_send(visc_copies())
    for p in range(chunks):
        if p + 2 >= chunks:
            wait_send(halo_copies(p))
            wait_mid_sent(p)
        wait_passed(p)
        for axis in ("gy", "gx"):
            for copy in sum_copies(p, axis)[0]:
                copy.wait_send()


def per_device(gx_n, gy_n, snapshots, viscosity, velocity):
    snaps, nx, ny, nz = snapshots.shape
    cells = nx * ny
    chunk = snaps // 4
    chunks = snaps // chunk
    f32 = jnp.float32
    dma = pltpu.SemaphoreType.DMA
    vmem = pl.BlockSpec(memory_space=pltpu.VMEM)
    modes, factor = pl.pallas_call(
        functools.partial(
            kernel, (snaps, nx, ny, nz), (gx_n, gy_n), chunk, float(cells * nz * gx_n * gy_n)
        ),
        out_shape=(
            jax.ShapeDtypeStruct((snaps * cells, nz), jnp.bfloat16),
            jax.ShapeDtypeStruct((snaps, snaps), f32),
        ),
        in_specs=[pl.BlockSpec(memory_space=pltpu.HBM)] * 3,
        out_specs=(vmem, vmem),
        scratch_shapes=[
            pltpu.VMEM((snaps * cells, nz), f32),
            pltpu.VMEM((nx, ny, nz), f32),
            pltpu.VMEM((3, nx, ny, nz), f32),
            dma((chunks,)), dma((2,)),
            pltpu.VMEM((chunks, nx + 4, ny + 4, chunk, nz), f32),
            pltpu.VMEM((chunks, 2, nx // 2, 2, chunk, nz), f32),
            pltpu.VMEM((4, nx, ny, nz), f32),
            pltpu.VMEM((nx + 2, ny + 2, nz), f32),
            pltpu.VMEM((3, 4, nx, ny, nz), f32),
            pltpu.VMEM((snaps, cells * nz), jnp.bfloat16),
            pltpu.VMEM((snaps, cells * nz), jnp.bfloat16),
            pltpu.VMEM((chunk * cells, nz), f32),
            pltpu.VMEM((chunks, gy_n, chunk, snaps), f32),
            pltpu.VMEM((chunks, gx_n, chunk, snaps), f32),
            pltpu.VMEM((snaps, snaps), f32),
            pltpu.VMEM((snaps, snaps), f32),
            pltpu.VMEM((snaps, snaps), f32),
            dma((chunks, 4)), dma((chunks, 4)), dma((chunks, 2)), dma((chunks, 2)), dma((chunks, 2)), dma((chunks, 2)),
            dma((4,)), dma((4,)),
            dma((chunks, gy_n)), dma((chunks, gy_n)), dma((chunks, gx_n)), dma((chunks, gx_n)),
        ],
        compiler_params=pltpu.CompilerParams(
            collective_id=0, has_side_effects=True, vmem_limit_bytes=51 * 1024 * 1024
        ),
        name="pod",
    )(snapshots.reshape(snaps * cells, nz), viscosity, velocity)
    return modes.reshape(snaps, nx, ny, nz), factor


def solution(mesh):
    placed = (P(None, "gx", "gy", None), P("gx", "gy", None), P(None, "gx", "gy", None))
    return jax.shard_map(
        functools.partial(per_device, mesh.shape["gx"], mesh.shape["gy"]),
        mesh=mesh,
        in_specs=placed,
        out_specs=(P(None, "gx", "gy", None), P()),
        check_vma=False,
    )
```

```python
import functools

import jax
import jax.numpy as jnp
from jax import lax
from jax.experimental import pallas as pl
from jax.experimental.pallas import tpu as pltpu
from jax.sharding import PartitionSpec as P

MESH = pl.DeviceIdType.MESH
HIGH = lax.Precision.HIGHEST


def dot(a, b, transposed=False):
    return lax.dot_general(
        a, b, (((1,), (1 if transposed else 0,)), ((), ())),
        precision=HIGH, preferred_element_type=jnp.float32,
    )


def narrow_dot(a, b, transposed=False):
    return lax.dot_general(
        a, b, (((1,), (1 if transposed else 0,)), ((), ())), preferred_element_type=jnp.float32
    )


def kernel(
    dims, peers, chunk, cells_total,
    snap_any, visc_any, vel_any, modes_ref, factor_ref,
    snap_ref, visc_ref, vel_ref, load_snap, load_rest, wide, passing, near_visc, pad_visc, coef, high, rest, rows_out, part_y, part_x, inv, low, diag,
    send_halo, recv_halo, send_mid, recv_pass, send_pass, recv_mid, send_visc, recv_visc, send_y, recv_y, send_x, recv_x,
):
    snaps, nx, ny, nz = dims
    gx_n, gy_n = peers
    cells = nx * ny
    chunks = snaps // chunk
    gx, gy = lax.axis_index("gx"), lax.axis_index("gy")

    def along_y(other):
        return {"gx": gx, "gy": other}

    def along_x(other):
        return {"gx": other, "gy": gy}

    def load(p):
        here = pl.ds(p * chunk * cells, chunk * cells)
        return pltpu.make_async_copy(snap_any.at[here], snap_ref.at[here], load_snap.at[p])

    load_visc = pltpu.make_async_copy(visc_any, visc_ref, load_rest.at[0])
    load_vel = pltpu.make_async_copy(vel_any, vel_ref, load_rest.at[1])
    load(0).start()
    load_visc.start()
    for p in range(1, chunks):
        load(p).start()
    load_vel.start()

    barrier = pltpu.get_barrier_semaphore()
    for off in range(1, gy_n):
        pl.semaphore_signal(barrier, inc=1, device_id=along_y(lax.rem(gy + off, gy_n)), device_id_type=MESH)
    for off in range(1, gx_n):
        pl.semaphore_signal(barrier, inc=1, device_id=along_x(lax.rem(gx + off, gx_n)), device_id_type=MESH)

    def spread(p):
        def plane(i, carry):
            for j in range(ny):
                wide[p, i + 2, j + 2] = snap_ref[
                    pl.ds(p * chunk * cells + i * ny + j, chunk, stride=cells), :
                ]
            return carry

        lax.fori_loop(0, nx, plane, 0)

    relayed = gy_n == 4
    if relayed:
        up_direct, down_direct = (gy == 0) | (gy == 2), (gy == 1) | (gy == 3)
        from_below, from_above = down_direct, up_direct
    else:
        up_direct, down_direct = gy < gy_n - 1, gy > 0
        from_below, from_above = gy > 0, gy < gy_n - 1
    half = nx // 2
    halves = (pl.ds(2, half), pl.ds(2 + half, half))
    mids = ((1, ny, 0, 0, (0, 3)), (2, 2, ny + 2, 1, (3, 0)))

    def first_hop(p, slot, h):
        _, row, _, _, relays = mids[slot]
        return pltpu.make_async_remote_copy(
            src_ref=wide.at[p, halves[h], pl.ds(row, 2)], dst_ref=passing.at[p, slot],
            send_sem=send_mid.at[p, int(h)], recv_sem=recv_pass.at[p, slot],
            device_id=along_y(relays[h]), device_id_type=MESH,
        )

    def first_hops(p, me):
        return [first_hop(p, me - 1, h) for h in (1, 0)]

    def second_hop(p, slot, relay):
        source, _, row, _, relays = mids[slot]
        h = relays.index(relay)
        return pltpu.make_async_remote_copy(
            src_ref=passing.at[p, slot], dst_ref=wide.at[p, halves[h], pl.ds(row, 2)],
            send_sem=send_pass.at[p, slot], recv_sem=recv_mid.at[p, h],
            device_id=along_y(3 - source), device_id_type=MESH,
        )

    def when_at(me, body):
        pl.when(gy == me)(body)

    def start_first(p):
        if relayed:
            for me in (1, 2):
                def go(me=me):
                    for copy in first_hops(p, me):
                        copy.start()
                when_at(me, go)

    def pass_on(p, late):
        if relayed:
            for relay in (0, 3):
                def go(relay=relay):
                    slot = (relay == 3) ^ (not late)
                    copy = second_hop(p, int(slot), relay)
                    first_hop(p, int(slot), mids[slot][4].index(relay)).wait_recv()
                    copy.start()
                when_at(relay, go)

    def wait_mid(p):
        if relayed:
            for me in (1, 2):
                def go(me=me):
                    for relay in mids[2 - me][4]:
                        second_hop(p, 2 - me, relay).wait_recv()
                when_at(me, go)

    def wait_mid_sent(p):
        if relayed:
            for me in (1, 2):
                def go(me=me):
                    for copy in first_hops(p, me):
                        copy.wait_send()
                when_at(me, go)

    def wait_passed(p):
        if relayed:
            for relay in (0, 3):
                def go(relay=relay):
                    for slot in range(2):
                        second_hop(p, slot, relay).wait_send()
                when_at(relay, go)

    def halo_copies(p):
        mid_x, mid_y = pl.ds(2, nx), pl.ds(2, ny)
        table = (
            (up_direct, along_y(gy + 1), (mid_x, pl.ds(ny, 2)), (mid_x, pl.ds(0, 2))),
            (down_direct, along_y(gy - 1), (mid_x, pl.ds(2, 2)), (mid_x, pl.ds(ny + 2, 2))),
            (gx < gx_n - 1, along_x(gx + 1), (pl.ds(nx, 2), mid_y), (pl.ds(0, 2), mid_y)),
            (gx > 0, along_x(gx - 1), (pl.ds(2, 2), mid_y), (pl.ds(nx + 2, 2), mid_y)),
        )
        return [
            (
                there,
                pltpu.make_async_remote_copy(
                    src_ref=wide.at[p, src[0], src[1]],
                    dst_ref=wide.at[p, dst[0], dst[1]],
                    send_sem=send_halo.at[p, way],
                    recv_sem=recv_halo.at[p, way],
                    device_id=who,
                    device_id_type=MESH,
                ),
            )
            for way, (there, who, src, dst) in enumerate(table)
        ]

    def visc_copies():
        table = (
            (gy < gy_n - 1, along_y(gy + 1)),
            (gy > 0, along_y(gy - 1)),
            (gx < gx_n - 1, along_x(gx + 1)),
            (gx > 0, along_x(gx - 1)),
        )
        return [
            (
                there,
                pltpu.make_async_remote_copy(
                    src_ref=visc_ref,
                    dst_ref=near_visc.at[way],
                    send_sem=send_visc.at[way],
                    recv_sem=recv_visc.at[way],
                    device_id=who,
                    device_id_type=MESH,
                ),
            )
            for way, (there, who) in enumerate(table)
        ]

    arrives = (gy > 0, gy < gy_n - 1, gx > 0, gx < gx_n - 1)
    arrives_direct = (from_below, from_above) + arrives[2:]

    def start(copies):
        for there, copy in copies:
            pl.when(there)(copy.start)

    def wait_recv(copies, comes):
        for way, (_, copy) in enumerate(copies):
            pl.when(comes[way])(copy.wait_recv)

    def wait_send(copies):
        for there, copy in copies:
            pl.when(there)(copy.wait_send)

    load(0).wait()
    spread(0)
    load_visc.wait()
    pl.semaphore_wait(barrier, gx_n + gy_n - 2)

    start(visc_copies())
    start_first(0)
    for p in range(1, chunks):
        load(p).wait()
        spread(p)
        if p < 3:
            start_first(p)
            start(halo_copies(p - 1))
    load_vel.wait()

    def border(way):
        rows_y = jnp.zeros((chunks, nx, 2, chunk, nz), jnp.float32)
        rows_x = jnp.zeros((chunks, 2, ny, chunk, nz), jnp.float32)
        if way == 0:
            wide[:, 2:nx + 2, 0:2] = rows_y
        elif way == 1:
            wide[:, 2:nx + 2, ny + 2:ny + 4] = rows_y
        elif way == 2:
            wide[:, 0:2, 2:ny + 2] = rows_x
        else:
            wide[:, nx + 2:nx + 4, 2:ny + 2] = rows_x

    for way in range(4):
        pl.when(jnp.logical_not(arrives[way]))(functools.partial(border, way))

    inv[...] = jnp.zeros_like(inv)
    pad_visc[...] = jnp.zeros_like(pad_visc)
    pad_visc[1:nx + 1, 1:ny + 1, :] = visc_ref[...]
    pass_on(0, False)
    pass_on(0, True)
    wait_recv(visc_copies(), arrives)

    def visc_border(way):
        if way == 0:
            pad_visc[1:nx + 1, 0:1, :] = near_visc[0, :, ny - 1:ny, :]
        elif way == 1:
            pad_visc[1:nx + 1, ny + 1:ny + 2, :] = near_visc[1, :, 0:1, :]
        elif way == 2:
            pad_visc[0:1, 1:ny + 1, :] = near_visc[2, nx - 1:nx, :, :]
        else:
            pad_visc[nx + 1:nx + 2, 1:ny + 1, :] = near_visc[3, 0:1, :, :]

    for way in range(4):
        pl.when(arrives[way])(functools.partial(visc_border, way))

    lane3 = lax.broadcasted_iota(jnp.int32, (nx, ny, nz), 2)
    mid = pad_visc[1:nx + 1, 1:ny + 1, :]
    around = (
        (pad_visc[2:nx + 2, 1:ny + 1, :], pad_visc[0:nx, 1:ny + 1, :]),
        (pad_visc[1:nx + 1, 2:ny + 2, :], pad_visc[1:nx + 1, 0:ny, :]),
        (
            jnp.where(lane3 < nz - 1, pltpu.roll(mid, nz - 1, 2), 0.0),
            jnp.where(lane3 > 0, pltpu.roll(mid, 1, 2), 0.0),
        ),
    )
    for d in range(3):
        coef[d, 0] = vel_ref[d] * (8.0 / 12.0)
        coef[d, 1] = vel_ref[d] * (1.0 / 12.0)
        coef[d, 2] = 0.5 * (mid + around[d][0])
        coef[d, 3] = 0.5 * (mid + around[d][1])

    lane = lax.broadcasted_iota(jnp.int32, (chunk, nz), 1)

    def stencil(p):
        def plane(i, carry):
            for j in range(ny):
                c = wide[p, i + 2, j + 2]
                near = (
                    (wide[p, i + 3, j + 2], wide[p, i + 1, j + 2], wide[p, i + 4, j + 2], wide[p, i, j + 2]),
                    (wide[p, i + 2, j + 3], wide[p, i + 2, j + 1], wide[p, i + 2, j + 4], wide[p, i + 2, j]),
                    (
                        jnp.where(lane < nz - 1, pltpu.roll(c, nz - 1, 1), 0.0),
                        jnp.where(lane > 0, pltpu.roll(c, 1, 1), 0.0),
                        jnp.where(lane < nz - 2, pltpu.roll(c, nz - 2, 1), 0.0),
                        jnp.where(lane > 1, pltpu.roll(c, 2, 1), 0.0),
                    ),
                )
                total = None
                for d in range(3):
                    up, down, up2, down2 = near[d]
                    w8, w1, vp, vm = (coef[d, t, i, pl.ds(j, 1), :] for t in range(4))
                    term = (w8 * (up - down) - w1 * (up2 - down2)) - (vp * (up - c) - vm * (c - down))
                    total = term if total is None else total + term
                lanes = pl.ds(pl.multiple_of((i * ny + j) * nz, nz), nz)
                upper = total.astype(jnp.bfloat16)
                high[pl.ds(p * chunk, chunk), lanes] = upper
                rest[pl.ds(p * chunk, chunk), lanes] = (total - upper.astype(jnp.float32)).astype(jnp.bfloat16)
            return carry

        lax.fori_loop(0, nx, plane, 0)

    def sum_copies(p, axis):
        me, count, who, part, send, recv = (
            (gy, gy_n, along_y, part_y, send_y, recv_y) if axis == "gy" else (gx, gx_n, along_x, part_x, send_x, recv_x)
        )
        out, into = [], []
        for off in range(1, count):
            to, frm = lax.rem(me + off, count), lax.rem(me + count - off, count)
            for list_, slot, k in ((out, me, to), (into, frm, frm)):
                list_.append(
                    pltpu.make_async_remote_copy(
                        src_ref=part.at[p, slot], dst_ref=part.at[p, slot],
                        send_sem=send.at[p, off], recv_sem=recv.at[p, off],
                        device_id=who(k), device_id_type=MESH,
                    )
                )
        return out, into

    def added(part, p, count):
        total = part[p, 0]
        for k in range(1, count):
            total = total + part[p, k]
        return total

    def halves_sum(with_high, with_rest):
        return with_high[:chunk] + (with_high[chunk:] + (with_rest[:chunk] + with_rest[chunk:]))

    def gram(p):
        top = (p + 1) * chunk
        both = jnp.concatenate([high[p * chunk:top, :], rest[p * chunk:top, :]], axis=0)
        panel = halves_sum(narrow_dot(both, high[0:top, :], True), narrow_dot(both, rest[0:top, :], True))
        panel = panel * (1.0 / cells_total)
        if top < snaps:
            panel = jnp.concatenate([panel, jnp.zeros((chunk, snaps - top), jnp.float32)], axis=1)
        part_y[p, gy] = panel
        for copy in sum_copies(p, "gy")[0]:
            copy.start()

    def gram_x(p):
        for copy in sum_copies(p, "gy")[1]:
            copy.wait_recv()
        part_x[p, gx] = added(part_y, p, gy_n)
        for copy in sum_copies(p, "gx")[0]:
            copy.start()

    row_s = lax.broadcasted_iota(jnp.int32, (chunk, snaps), 0)
    lane_s = lax.broadcasted_iota(jnp.int32, (chunk, snaps), 1)

    def padded(x):
        return x if chunk == snaps else jnp.concatenate([x, jnp.zeros((snaps - chunk, snaps), jnp.float32)], axis=0)

    def factor(p):
        for copy in sum_copies(p, "gx")[1]:
            copy.wait_recv()
        g = added(part_x, p, gx_n)
        w0 = p * chunk
        here = pl.ds(w0, chunk)
        if p > 0:
            off = dot(g, inv[...], transposed=True)
            g = pltpu.roll(g, snaps - w0, 1) - dot(off, padded(off), transposed=True)
            back = dot(off, inv[...])
            low[here, :] = off
        else:
            low[here, :] = jnp.zeros((chunk, snaps), jnp.float32)
        a = jnp.where(lane_s < chunk, g, jnp.where(lane_s == row_s + chunk, 1.0, 0.0))
        step = 8
        a = a.reshape(chunk // step, step, snaps)
        row_8 = lax.broadcasted_iota(jnp.int32, (step, snaps), 0)

        def splat(x, row):
            return jnp.broadcast_to(x[row:row + 1, :], (step, snaps))

        done = []
        for block in range(chunk // step):
            first = block * step
            own_rows, later = a[0], a[1:]
            columns = [jnp.broadcast_to(later[:, :, first + t:first + t + 1], later.shape) for t in range(step)]
            own_cols = [jnp.broadcast_to(own_rows[:, first + t:first + t + 1], (step, snaps)) for t in range(step)]
            entries = {(t, u): splat(own_cols[t], u) for t in range(step) for u in range(t, step)}
            rows = [splat(own_rows, t) for t in range(step)]
            for t in range(step):
                over = 1.0 / entries[t, t]
                scaled = rows[t] * over
                if later.shape[0]:
                    later = later - columns[t] * scaled[None]
                for u in range(t + 1, step):
                    ratio = entries[t, u] * over
                    for v in range(u, step):
                        entries[u, v] = entries[u, v] - ratio * entries[t, v]
                    rows[u] = rows[u] - ratio * rows[t]
                    if later.shape[0]:
                        columns[u] = columns[u] - columns[t] * ratio[None]
            kept = rows[0]
            for t in range(1, step):
                kept = jnp.where(row_8 == t, rows[t], kept)
            done.append(kept)
            a = later
        a = jnp.concatenate(done, axis=0)
        pivots = jnp.sum(jnp.where(lane_s == row_s, a, 0.0), axis=1, keepdims=True)
        a = a / jnp.sqrt(pivots)
        upper = jnp.where((lane_s >= row_s) & (lane_s < chunk), a, 0.0)
        own = jnp.where(lane_s < chunk, pltpu.roll(a, snaps - chunk, 1), 0.0)
        if p > 0:
            diag[here, :] = pltpu.roll(upper, w0, 1)
            inv[here, :] = pltpu.roll(own, w0, 1) - dot(own, padded(back))
        else:
            diag[here, :] = upper
            inv[here, :] = own

    def modes(p):
        top = (p + 1) * chunk
        full = inv[p * chunk:top, 0:top]
        upper = full.astype(jnp.bfloat16)
        weights = jnp.concatenate([upper, (full - upper.astype(jnp.float32)).astype(jnp.bfloat16)], axis=0)

        def plane(i, carry):
            first = pl.multiple_of(i * ny * nz, ny * nz)
            lanes = pl.ds(first, ny * nz)
            block = halves_sum(narrow_dot(weights, high[0:top, lanes]), narrow_dot(weights, rest[0:top, lanes]))
            for j in range(ny):
                rows_out[pl.ds(i * ny + j, chunk, stride=cells), :] = block[:, j * nz:(j + 1) * nz]
            return carry

        lax.fori_loop(0, nx, plane, 0)
        modes_ref[p * chunk * cells:top * cells, :] = rows_out[...].astype(jnp.bfloat16)

    for p in range(chunks):
        if p == 0:
            pass_on(1, False)
            pass_on(1, True)
        wait_recv(halo_copies(p), arrives_direct)
        wait_mid(p)
        if p + 2 < chunks:
            if p + 3 < chunks:
                start_first(p + 3)
            wait_send(halo_copies(p))
            start(halo_copies(p + 2))
        stencil(p)
        gram(p)
        if p + 2 < chunks:
            pass_on(p + 2, False)
            pass_on(p + 2, True)
        if p > 0:
            factor(p - 1)
        gram_x(p)
        if p > 0:
            modes(p - 1)
    factor(chunks - 1)
    modes(chunks - 1)
    factor_ref[...] = low[...].T + diag[...]

    wait_send(visc_copies())
    for p in range(chunks):
        if p + 2 >= chunks:
            wait_send(halo_copies(p))
        wait_mid_sent(p)
        wait_passed(p)
        for axis in ("gy", "gx"):
            for copy in sum_copies(p, axis)[0]:
                copy.wait_send()


def per_device(gx_n, gy_n, snapshots, viscosity, velocity):
    snaps, nx, ny, nz = snapshots.shape
    cells = nx * ny
    chunk = snaps // 4
    chunks = snaps // chunk
    f32 = jnp.float32
    dma = pltpu.SemaphoreType.DMA
    vmem = pl.BlockSpec(memory_space=pltpu.VMEM)
    modes, factor = pl.pallas_call(
        functools.partial(
            kernel, (snaps, nx, ny, nz), (gx_n, gy_n), chunk, float(cells * nz * gx_n * gy_n)
        ),
        out_shape=(
            jax.ShapeDtypeStruct((snaps * cells, nz), jnp.bfloat16),
            jax.ShapeDtypeStruct((snaps, snaps), f32),
        ),
        in_specs=[pl.BlockSpec(memory_space=pltpu.HBM)] * 3,
        out_specs=(vmem, vmem),
        scratch_shapes=[
            pltpu.VMEM((snaps * cells, nz), f32),
            pltpu.VMEM((nx, ny, nz), f32),
            pltpu.VMEM((3, nx, ny, nz), f32),
            dma((chunks,)), dma((2,)),
            pltpu.VMEM((chunks, nx + 4, ny + 4, chunk, nz), f32),
            pltpu.VMEM((chunks, 2, nx // 2, 2, chunk, nz), f32),
            pltpu.VMEM((4, nx, ny, nz), f32),
            pltpu.VMEM((nx + 2, ny + 2, nz), f32),
            pltpu.VMEM((3, 4, nx, ny, nz), f32),
            pltpu.VMEM((snaps, cells * nz), jnp.bfloat16),
            pltpu.VMEM((snaps, cells * nz), jnp.bfloat16),
            pltpu.VMEM((chunk * cells, nz), f32),
            pltpu.VMEM((chunks, gy_n, chunk, snaps), f32),
            pltpu.VMEM((chunks, gx_n, chunk, snaps), f32),
            pltpu.VMEM((snaps, snaps), f32),
            pltpu.VMEM((snaps, snaps), f32),
            pltpu.VMEM((snaps, snaps), f32),
            dma((chunks, 4)), dma((chunks, 4)), dma((chunks, 2)), dma((chunks, 2)), dma((chunks, 2)), dma((chunks, 2)),
            dma((4,)), dma((4,)),
            dma((chunks, gy_n)), dma((chunks, gy_n)), dma((chunks, gx_n)), dma((chunks, gx_n)),
        ],
        compiler_params=pltpu.CompilerParams(
            collective_id=0, has_side_effects=True, vmem_limit_bytes=51 * 1024 * 1024
        ),
        name="pod",
    )(snapshots.reshape(snaps * cells, nz), viscosity, velocity)
    return modes.reshape(snaps, nx, ny, nz), factor


def solution(mesh):
    placed = (P(None, "gx", "gy", None), P("gx", "gy", None), P(None, "gx", "gy", None))
    return jax.shard_map(
        functools.partial(per_device, mesh.shape["gx"], mesh.shape["gy"]),
        mesh=mesh,
        in_specs=placed,
        out_specs=(P(None, "gx", "gy", None), P()),
        check_vma=False,
    )
```

```python
import functools

import jax
import jax.numpy as jnp
from jax import lax
from jax.experimental import pallas as pl
from jax.experimental.pallas import tpu as pltpu
from jax.sharding import PartitionSpec as P

MESH = pl.DeviceIdType.MESH
HIGH = lax.Precision.HIGHEST


def dot(a, b, transposed=False):
    return lax.dot_general(
        a, b, (((1,), (1 if transposed else 0,)), ((), ())),
        precision=HIGH, preferred_element_type=jnp.float32,
    )


def narrow_dot(a, b, transposed=False):
    return lax.dot_general(
        a, b, (((1,), (1 if transposed else 0,)), ((), ())), preferred_element_type=jnp.float32
    )


def kernel(
    dims, peers, chunk, cells_total,
    snap_any, visc_any, vel_any, modes_ref, factor_ref,
    snap_ref, visc_ref, vel_ref, load_snap, load_rest, wide, passing, near_visc, pad_visc, coef, high, rest, rows_out, part_y, part_x, inv, low, diag,
    send_halo, recv_halo, send_mid, recv_pass, send_pass, recv_mid, send_visc, recv_visc, send_y, recv_y, send_x, recv_x,
):
    snaps, nx, ny, nz = dims
    gx_n, gy_n = peers
    cells = nx * ny
    chunks = snaps // chunk
    gx, gy = lax.axis_index("gx"), lax.axis_index("gy")

    def along_y(other):
        return {"gx": gx, "gy": other}

    def along_x(other):
        return {"gx": other, "gy": gy}

    def load(p):
        here = pl.ds(p * chunk * cells, chunk * cells)
        return pltpu.make_async_copy(snap_any.at[here], snap_ref.at[here], load_snap.at[p])

    load_visc = pltpu.make_async_copy(visc_any, visc_ref, load_rest.at[0])
    load_vel = pltpu.make_async_copy(vel_any, vel_ref, load_rest.at[1])
    load(0).start()
    load_visc.start()
    for p in range(1, chunks):
        load(p).start()
    load_vel.start()

    barrier = pltpu.get_barrier_semaphore()
    for off in range(1, gy_n):
        pl.semaphore_signal(barrier, inc=1, device_id=along_y(lax.rem(gy + off, gy_n)), device_id_type=MESH)
    for off in range(1, gx_n):
        pl.semaphore_signal(barrier, inc=1, device_id=along_x(lax.rem(gx + off, gx_n)), device_id_type=MESH)

    def spread(p):
        def plane(i, carry):
            for j in range(ny):
                wide[p, i + 2, j + 2] = snap_ref[
                    pl.ds(p * chunk * cells + i * ny + j, chunk, stride=cells), :
                ]
            return carry

        lax.fori_loop(0, nx, plane, 0)

    relayed = gy_n == 4
    if relayed:
        up_direct, down_direct = (gy == 0) | (gy == 2), (gy == 1) | (gy == 3)
        from_below, from_above = down_direct, up_direct
    else:
        up_direct, down_direct = gy < gy_n - 1, gy > 0
        from_below, from_above = gy > 0, gy < gy_n - 1
    half = nx // 2
    halves = (pl.ds(2, half), pl.ds(2 + half, half))
    mids = ((1, ny, 0, 0, (0, 3)), (2, 2, ny + 2, 1, (3, 0)))

    def first_hop(p, slot, h):
        _, row, _, _, relays = mids[slot]
        return pltpu.make_async_remote_copy(
            src_ref=wide.at[p, halves[h], pl.ds(row, 2)], dst_ref=passing.at[p, slot],
            send_sem=send_mid.at[p, int(h)], recv_sem=recv_pass.at[p, slot],
            device_id=along_y(relays[h]), device_id_type=MESH,
        )

    def first_hops(p, me):
        return [first_hop(p, me - 1, h) for h in (1, 0)]

    def second_hop(p, slot, relay):
        source, _, row, _, relays = mids[slot]
        h = relays.index(relay)
        return pltpu.make_async_remote_copy(
            src_ref=passing.at[p, slot], dst_ref=wide.at[p, halves[h], pl.ds(row, 2)],
            send_sem=send_pass.at[p, slot], recv_sem=recv_mid.at[p, h],
            device_id=along_y(3 - source), device_id_type=MESH,
        )

    def when_at(me, body):
        pl.when(gy == me)(body)

    def start_first(p):
        if relayed:
            for me in (1, 2):
                def go(me=me):
                    for copy in first_hops(p, me):
                        copy.start()
                when_at(me, go)

    def pass_on(p, late):
        if relayed:
            for relay in (0, 3):
                def go(relay=relay):
                    slot = (relay == 3) ^ (not late)
                    copy = second_hop(p, int(slot), relay)
                    first_hop(p, int(slot), mids[slot][4].index(relay)).wait_recv()
                    copy.start()
                when_at(relay, go)

    def wait_mid(p):
        if relayed:
            for me in (1, 2):
                def go(me=me):
                    for relay in mids[2 - me][4]:
                        second_hop(p, 2 - me, relay).wait_recv()
                when_at(me, go)

    def wait_mid_sent(p):
        if relayed:
            for me in (1, 2):
                def go(me=me):
                    for copy in first_hops(p, me):
                        copy.wait_send()
                when_at(me, go)

    def wait_passed(p):
        if relayed:
            for relay in (0, 3):
                def go(relay=relay):
                    for slot in range(2):
                        second_hop(p, slot, relay).wait_send()
                when_at(relay, go)

    def halo_copies(p):
        mid_x, mid_y = pl.ds(2, nx), pl.ds(2, ny)
        table = (
            (up_direct, along_y(gy + 1), (mid_x, pl.ds(ny, 2)), (mid_x, pl.ds(0, 2))),
            (down_direct, along_y(gy - 1), (mid_x, pl.ds(2, 2)), (mid_x, pl.ds(ny + 2, 2))),
            (gx < gx_n - 1, along_x(gx + 1), (pl.ds(nx, 2), mid_y), (pl.ds(0, 2), mid_y)),
            (gx > 0, along_x(gx - 1), (pl.ds(2, 2), mid_y), (pl.ds(nx + 2, 2), mid_y)),
        )
        return [
            (
                there,
                pltpu.make_async_remote_copy(
                    src_ref=wide.at[p, src[0], src[1]],
                    dst_ref=wide.at[p, dst[0], dst[1]],
                    send_sem=send_halo.at[p, way],
                    recv_sem=recv_halo.at[p, way],
                    device_id=who,
                    device_id_type=MESH,
                ),
            )
            for way, (there, who, src, dst) in enumerate(table)
        ]

    def visc_copies():
        table = (
            (gy < gy_n - 1, along_y(gy + 1)),
            (gy > 0, along_y(gy - 1)),
            (gx < gx_n - 1, along_x(gx + 1)),
            (gx > 0, along_x(gx - 1)),
        )
        return [
            (
                there,
                pltpu.make_async_remote_copy(
                    src_ref=visc_ref,
                    dst_ref=near_visc.at[way],
                    send_sem=send_visc.at[way],
                    recv_sem=recv_visc.at[way],
                    device_id=who,
                    device_id_type=MESH,
                ),
            )
            for way, (there, who) in enumerate(table)
        ]

    arrives = (gy > 0, gy < gy_n - 1, gx > 0, gx < gx_n - 1)
    arrives_direct = (from_below, from_above) + arrives[2:]

    def start(copies):
        for there, copy in copies:
            pl.when(there)(copy.start)

    def wait_recv(copies, comes):
        for way, (_, copy) in enumerate(copies):
            pl.when(comes[way])(copy.wait_recv)

    def wait_send(copies):
        for there, copy in copies:
            pl.when(there)(copy.wait_send)

    load(0).wait()
    spread(0)
    load_visc.wait()
    pl.semaphore_wait(barrier, gx_n + gy_n - 2)

    start(visc_copies())
    start_first(0)
    for p in range(1, chunks):
        load(p).wait()
        spread(p)
        if p == 1:
            start(halo_copies(0))
            start_first(1)
    load_vel.wait()

    def border(way):
        rows_y = jnp.zeros((chunks, nx, 2, chunk, nz), jnp.float32)
        rows_x = jnp.zeros((chunks, 2, ny, chunk, nz), jnp.float32)
        if way == 0:
            wide[:, 2:nx + 2, 0:2] = rows_y
        elif way == 1:
            wide[:, 2:nx + 2, ny + 2:ny + 4] = rows_y
        elif way == 2:
            wide[:, 0:2, 2:ny + 2] = rows_x
        else:
            wide[:, nx + 2:nx + 4, 2:ny + 2] = rows_x

    for way in range(4):
        pl.when(jnp.logical_not(arrives[way]))(functools.partial(border, way))

    inv[...] = jnp.zeros_like(inv)
    pad_visc[...] = jnp.zeros_like(pad_visc)
    pad_visc[1:nx + 1, 1:ny + 1, :] = visc_ref[...]
    pass_on(0, False)
    pass_on(0, True)
    wait_recv(visc_copies(), arrives)

    def visc_border(way):
        if way == 0:
            pad_visc[1:nx + 1, 0:1, :] = near_visc[0, :, ny - 1:ny, :]
        elif way == 1:
            pad_visc[1:nx + 1, ny + 1:ny + 2, :] = near_visc[1, :, 0:1, :]
        elif way == 2:
            pad_visc[0:1, 1:ny + 1, :] = near_visc[2, nx - 1:nx, :, :]
        else:
            pad_visc[nx + 1:nx + 2, 1:ny + 1, :] = near_visc[3, 0:1, :, :]

    for way in range(4):
        pl.when(arrives[way])(functools.partial(visc_border, way))

    lane3 = lax.broadcasted_iota(jnp.int32, (nx, ny, nz), 2)
    mid = pad_visc[1:nx + 1, 1:ny + 1, :]
    around = (
        (pad_visc[2:nx + 2, 1:ny + 1, :], pad_visc[0:nx, 1:ny + 1, :]),
        (pad_visc[1:nx + 1, 2:ny + 2, :], pad_visc[1:nx + 1, 0:ny, :]),
        (
            jnp.where(lane3 < nz - 1, pltpu.roll(mid, nz - 1, 2), 0.0),
            jnp.where(lane3 > 0, pltpu.roll(mid, 1, 2), 0.0),
        ),
    )
    for d in range(3):
        coef[d, 0] = vel_ref[d] * (8.0 / 12.0)
        coef[d, 1] = vel_ref[d] * (1.0 / 12.0)
        coef[d, 2] = 0.5 * (mid + around[d][0])
        coef[d, 3] = 0.5 * (mid + around[d][1])

    lane = lax.broadcasted_iota(jnp.int32, (chunk, nz), 1)

    def stencil(p):
        def plane(i, carry):
            for j in range(ny):
                c = wide[p, i + 2, j + 2]
                near = (
                    (wide[p, i + 3, j + 2], wide[p, i + 1, j + 2], wide[p, i + 4, j + 2], wide[p, i, j + 2]),
                    (wide[p, i + 2, j + 3], wide[p, i + 2, j + 1], wide[p, i + 2, j + 4], wide[p, i + 2, j]),
                    (
                        jnp.where(lane < nz - 1, pltpu.roll(c, nz - 1, 1), 0.0),
                        jnp.where(lane > 0, pltpu.roll(c, 1, 1), 0.0),
                        jnp.where(lane < nz - 2, pltpu.roll(c, nz - 2, 1), 0.0),
                        jnp.where(lane > 1, pltpu.roll(c, 2, 1), 0.0),
                    ),
                )
                total = None
                for d in range(3):
                    up, down, up2, down2 = near[d]
                    w8, w1, vp, vm = (coef[d, t, i, pl.ds(j, 1), :] for t in range(4))
                    term = (w8 * (up - down) - w1 * (up2 - down2)) - (vp * (up - c) - vm * (c - down))
                    total = term if total is None else total + term
                lanes = pl.ds(pl.multiple_of((i * ny + j) * nz, nz), nz)
                upper = total.astype(jnp.bfloat16)
                high[pl.ds(p * chunk, chunk), lanes] = upper
                rest[pl.ds(p * chunk, chunk), lanes] = (total - upper.astype(jnp.float32)).astype(jnp.bfloat16)
            return carry

        lax.fori_loop(0, nx, plane, 0)

    def sum_copies(p, axis):
        me, count, who, part, send, recv = (
            (gy, gy_n, along_y, part_y, send_y, recv_y) if axis == "gy" else (gx, gx_n, along_x, part_x, send_x, recv_x)
        )
        out, into = [], []
        for off in range(1, count):
            to, frm = lax.rem(me + off, count), lax.rem(me + count - off, count)
            for list_, slot, k in ((out, me, to), (into, frm, frm)):
                list_.append(
                    pltpu.make_async_remote_copy(
                        src_ref=part.at[p, slot], dst_ref=part.at[p, slot],
                        send_sem=send.at[p, off], recv_sem=recv.at[p, off],
                        device_id=who(k), device_id_type=MESH,
                    )
                )
        return out, into

    def added(part, p, count):
        total = part[p, 0]
        for k in range(1, count):
            total = total + part[p, k]
        return total

    def halves_sum(with_high, with_rest):
        return with_high[:chunk] + (with_high[chunk:] + (with_rest[:chunk] + with_rest[chunk:]))

    def gram(p):
        top = (p + 1) * chunk
        both = jnp.concatenate([high[p * chunk:top, :], rest[p * chunk:top, :]], axis=0)
        panel = halves_sum(narrow_dot(both, high[0:top, :], True), narrow_dot(both, rest[0:top, :], True))
        panel = panel * (1.0 / cells_total)
        if top < snaps:
            panel = jnp.concatenate([panel, jnp.zeros((chunk, snaps - top), jnp.float32)], axis=1)
        part_y[p, gy] = panel
        for copy in sum_copies(p, "gy")[0]:
            copy.start()

    def gram_x(p):
        for copy in sum_copies(p, "gy")[1]:
            copy.wait_recv()
        part_x[p, gx] = added(part_y, p, gy_n)
        for copy in sum_copies(p, "gx")[0]:
            copy.start()

    row_s = lax.broadcasted_iota(jnp.int32, (chunk, snaps), 0)
    lane_s = lax.broadcasted_iota(jnp.int32, (chunk, snaps), 1)

    def padded(x):
        return x if chunk == snaps else jnp.concatenate([x, jnp.zeros((snaps - chunk, snaps), jnp.float32)], axis=0)

    def factor(p):
        for copy in sum_copies(p, "gx")[1]:
            copy.wait_recv()
        g = added(part_x, p, gx_n)
        w0 = p * chunk
        here = pl.ds(w0, chunk)
        if p > 0:
            off = dot(g, inv[...], transposed=True)
            g = pltpu.roll(g, snaps - w0, 1) - dot(off, padded(off), transposed=True)
            back = dot(off, inv[...])
            low[here, :] = off
        else:
            low[here, :] = jnp.zeros((chunk, snaps), jnp.float32)
        a = jnp.where(lane_s < chunk, g, jnp.where(lane_s == row_s + chunk, 1.0, 0.0))
        step = 8
        a = a.reshape(chunk // step, step, snaps)
        row_8 = lax.broadcasted_iota(jnp.int32, (step, snaps), 0)

        def splat(x, row):
            return jnp.broadcast_to(x[row:row + 1, :], (step, snaps))

        done = []
        for block in range(chunk // step):
            first = block * step
            own_rows, later = a[0], a[1:]
            columns = [jnp.broadcast_to(later[:, :, first + t:first + t + 1], later.shape) for t in range(step)]
            own_cols = [jnp.broadcast_to(own_rows[:, first + t:first + t + 1], (step, snaps)) for t in range(step)]
            entries = {(t, u): splat(own_cols[t], u) for t in range(step) for u in range(t, step)}
            rows = [splat(own_rows, t) for t in range(step)]
            for t in range(step):
                over = 1.0 / entries[t, t]
                scaled = rows[t] * over
                if later.shape[0]:
                    later = later - columns[t] * scaled[None]
                for u in range(t + 1, step):
                    ratio = entries[t, u] * over
                    for v in range(u, step):
                        entries[u, v] = entries[u, v] - ratio * entries[t, v]
                    rows[u] = rows[u] - ratio * rows[t]
                    if later.shape[0]:
                        columns[u] = columns[u] - columns[t] * ratio[None]
            kept = rows[0]
            for t in range(1, step):
                kept = jnp.where(row_8 == t, rows[t], kept)
            done.append(kept)
            a = later
        a = jnp.concatenate(done, axis=0)
        pivots = jnp.sum(jnp.where(lane_s == row_s, a, 0.0), axis=1, keepdims=True)
        a = a / jnp.sqrt(pivots)
        upper = jnp.where((lane_s >= row_s) & (lane_s < chunk), a, 0.0)
        own = jnp.where(lane_s < chunk, pltpu.roll(a, snaps - chunk, 1), 0.0)
        if p > 0:
            diag[here, :] = pltpu.roll(upper, w0, 1)
            inv[here, :] = pltpu.roll(own, w0, 1) - dot(own, padded(back))
        else:
            diag[here, :] = upper
            inv[here, :] = own

    def modes(p):
        top = (p + 1) * chunk
        full = inv[p * chunk:top, 0:top]
        upper = full.astype(jnp.bfloat16)
        weights = jnp.concatenate([upper, (full - upper.astype(jnp.float32)).astype(jnp.bfloat16)], axis=0)

        def plane(i, carry):
            first = pl.multiple_of(i * ny * nz, ny * nz)
            lanes = pl.ds(first, ny * nz)
            block = halves_sum(narrow_dot(weights, high[0:top, lanes]), narrow_dot(weights, rest[0:top, lanes]))
            for j in range(ny):
                rows_out[pl.ds(i * ny + j, chunk, stride=cells), :] = block[:, j * nz:(j + 1) * nz]
            return carry

        lax.fori_loop(0, nx, plane, 0)
        modes_ref[p * chunk * cells:top * cells, :] = rows_out[...].astype(jnp.bfloat16)

    for p in range(chunks):
        wait_send(halo_copies(p))
        if p + 1 < chunks:
            start(halo_copies(p + 1))
        if p + 2 < chunks:
            start_first(p + 2)
        if p + 1 < chunks:
            pass_on(p + 1, False)
            pass_on(p + 1, True)
        wait_recv(halo_copies(p), arrives_direct)
        wait_mid(p)
        stencil(p)
        gram(p)
        if p > 0:
            factor(p - 1)
        gram_x(p)
        if p > 0:
            modes(p - 1)
    factor(chunks - 1)
    modes(chunks - 1)
    factor_ref[...] = low[...].T + diag[...]

    wait_send(visc_copies())
    for p in range(chunks):
        wait_mid_sent(p)
        wait_passed(p)
        for axis in ("gy", "gx"):
            for copy in sum_copies(p, axis)[0]:
                copy.wait_send()


def per_device(gx_n, gy_n, snapshots, viscosity, velocity):
    snaps, nx, ny, nz = snapshots.shape
    cells = nx * ny
    chunk = snaps // 4
    chunks = snaps // chunk
    f32 = jnp.float32
    dma = pltpu.SemaphoreType.DMA
    vmem = pl.BlockSpec(memory_space=pltpu.VMEM)
    modes, factor = pl.pallas_call(
        functools.partial(
            kernel, (snaps, nx, ny, nz), (gx_n, gy_n), chunk, float(cells * nz * gx_n * gy_n)
        ),
        out_shape=(
            jax.ShapeDtypeStruct((snaps * cells, nz), jnp.bfloat16),
            jax.ShapeDtypeStruct((snaps, snaps), f32),
        ),
        in_specs=[pl.BlockSpec(memory_space=pltpu.HBM)] * 3,
        out_specs=(vmem, vmem),
        scratch_shapes=[
            pltpu.VMEM((snaps * cells, nz), f32),
            pltpu.VMEM((nx, ny, nz), f32),
            pltpu.VMEM((3, nx, ny, nz), f32),
            dma((chunks,)), dma((2,)),
            pltpu.VMEM((chunks, nx + 4, ny + 4, chunk, nz), f32),
            pltpu.VMEM((chunks, 2, nx // 2, 2, chunk, nz), f32),
            pltpu.VMEM((4, nx, ny, nz), f32),
            pltpu.VMEM((nx + 2, ny + 2, nz), f32),
            pltpu.VMEM((3, 4, nx, ny, nz), f32),
            pltpu.VMEM((snaps, cells * nz), jnp.bfloat16),
            pltpu.VMEM((snaps, cells * nz), jnp.bfloat16),
            pltpu.VMEM((chunk * cells, nz), f32),
            pltpu.VMEM((chunks, gy_n, chunk, snaps), f32),
            pltpu.VMEM((chunks, gx_n, chunk, snaps), f32),
            pltpu.VMEM((snaps, snaps), f32),
            pltpu.VMEM((snaps, snaps), f32),
            pltpu.VMEM((snaps, snaps), f32),
            dma((chunks, 4)), dma((chunks, 4)), dma((chunks, 2)), dma((chunks, 2)), dma((chunks, 2)), dma((chunks, 2)),
            dma((4,)), dma((4,)),
            dma((chunks, gy_n)), dma((chunks, gy_n)), dma((chunks, gx_n)), dma((chunks, gx_n)),
        ],
        compiler_params=pltpu.CompilerParams(
            collective_id=0, has_side_effects=True, vmem_limit_bytes=51 * 1024 * 1024
        ),
        name="pod",
    )(snapshots.reshape(snaps * cells, nz), viscosity, velocity)
    return modes.reshape(snaps, nx, ny, nz), factor


def solution(mesh):
    placed = (P(None, "gx", "gy", None), P("gx", "gy", None), P(None, "gx", "gy", None))
    return jax.shard_map(
        functools.partial(per_device, mesh.shape["gx"], mesh.shape["gy"]),
        mesh=mesh,
        in_specs=placed,
        out_specs=(P(None, "gx", "gy", None), P()),
        check_vma=False,
    )
```

```python
import functools

import jax
import jax.numpy as jnp
from jax import lax
from jax.experimental import pallas as pl
from jax.experimental.pallas import tpu as pltpu
from jax.sharding import PartitionSpec as P

MESH = pl.DeviceIdType.MESH
HIGH = lax.Precision.HIGHEST


def dot(a, b, transposed=False):
    return lax.dot_general(
        a, b, (((1,), (1 if transposed else 0,)), ((), ())),
        precision=HIGH, preferred_element_type=jnp.float32,
    )


def narrow_dot(a, b, transposed=False):
    return lax.dot_general(
        a, b, (((1,), (1 if transposed else 0,)), ((), ())), preferred_element_type=jnp.float32
    )


def kernel(
    dims, peers, chunk, cells_total,
    snap_any, visc_any, vel_any, modes_ref, factor_ref,
    snap_ref, visc_ref, vel_ref, load_snap, load_rest, wide, passing, near_visc, pad_visc, coef, high, rest, rows_out, part_y, part_x, inv, low, diag,
    send_halo, recv_halo, send_mid, recv_pass, send_pass, recv_mid, send_visc, recv_visc, send_y, recv_y, send_x, recv_x,
):
    snaps, nx, ny, nz = dims
    gx_n, gy_n = peers
    cells = nx * ny
    chunks = snaps // chunk
    gx, gy = lax.axis_index("gx"), lax.axis_index("gy")

    def along_y(other):
        return {"gx": gx, "gy": other}

    def along_x(other):
        return {"gx": other, "gy": gy}

    def load(p):
        here = pl.ds(p * chunk * cells, chunk * cells)
        return pltpu.make_async_copy(snap_any.at[here], snap_ref.at[here], load_snap.at[p])

    load_visc = pltpu.make_async_copy(visc_any, visc_ref, load_rest.at[0])
    load_vel = pltpu.make_async_copy(vel_any, vel_ref, load_rest.at[1])
    load(0).start()
    load_visc.start()
    for p in range(1, chunks):
        load(p).start()
    load_vel.start()

    barrier = pltpu.get_barrier_semaphore()
    for off in range(1, gy_n):
        pl.semaphore_signal(barrier, inc=1, device_id=along_y(lax.rem(gy + off, gy_n)), device_id_type=MESH)
    for off in range(1, gx_n):
        pl.semaphore_signal(barrier, inc=1, device_id=along_x(lax.rem(gx + off, gx_n)), device_id_type=MESH)

    def spread(p):
        def plane(i, carry):
            for j in range(ny):
                wide[p, i + 2, j + 2] = snap_ref[
                    pl.ds(p * chunk * cells + i * ny + j, chunk, stride=cells), :
                ]
            return carry

        lax.fori_loop(0, nx, plane, 0)

    relayed = gy_n == 4
    if relayed:
        up_direct, down_direct = (gy == 0) | (gy == 2), (gy == 1) | (gy == 3)
        from_below, from_above = down_direct, up_direct
    else:
        up_direct, down_direct = gy < gy_n - 1, gy > 0
        from_below, from_above = gy > 0, gy < gy_n - 1
    half = nx // 2
    halves = (pl.ds(2, half), pl.ds(2 + half, half))
    mids = ((1, ny, 0, 0, (0, 3)), (2, 2, ny + 2, 1, (3, 0)))

    def first_hop(p, slot, h):
        _, row, _, _, relays = mids[slot]
        return pltpu.make_async_remote_copy(
            src_ref=wide.at[p, halves[h], pl.ds(row, 2)], dst_ref=passing.at[p, slot],
            send_sem=send_mid.at[p, int(h)], recv_sem=recv_pass.at[p, slot],
            device_id=along_y(relays[h]), device_id_type=MESH,
        )

    def first_hops(p, me):
        return [first_hop(p, me - 1, h) for h in (1, 0)]

    def second_hop(p, slot, relay):
        source, _, row, _, relays = mids[slot]
        h = relays.index(relay)
        return pltpu.make_async_remote_copy(
            src_ref=passing.at[p, slot], dst_ref=wide.at[p, halves[h], pl.ds(row, 2)],
            send_sem=send_pass.at[p, slot], recv_sem=recv_mid.at[p, h],
            device_id=along_y(3 - source), device_id_type=MESH,
        )

    def when_at(me, body):
        pl.when(gy == me)(body)

    def start_first(p):
        if relayed:
            for me in (1, 2):
                def go(me=me):
                    for copy in first_hops(p, me):
                        copy.start()
                when_at(me, go)

    def pass_on(p, late):
        if relayed:
            for relay in (0, 3):
                def go(relay=relay):
                    slot = (relay == 3) ^ (not late)
                    copy = second_hop(p, int(slot), relay)
                    first_hop(p, int(slot), mids[slot][4].index(relay)).wait_recv()
                    copy.start()
                when_at(relay, go)

    def wait_mid(p):
        if relayed:
            for me in (1, 2):
                def go(me=me):
                    for relay in mids[2 - me][4]:
                        second_hop(p, 2 - me, relay).wait_recv()
                when_at(me, go)

    def wait_mid_sent(p):
        if relayed:
            for me in (1, 2):
                def go(me=me):
                    for copy in first_hops(p, me):
                        copy.wait_send()
                when_at(me, go)

    def wait_passed(p):
        if relayed:
            for relay in (0, 3):
                def go(relay=relay):
                    for slot in range(2):
                        second_hop(p, slot, relay).wait_send()
                when_at(relay, go)

    def halo_copies(p):
        mid_x, mid_y = pl.ds(2, nx), pl.ds(2, ny)
        table = (
            (up_direct, along_y(gy + 1), (mid_x, pl.ds(ny, 2)), (mid_x, pl.ds(0, 2))),
            (down_direct, along_y(gy - 1), (mid_x, pl.ds(2, 2)), (mid_x, pl.ds(ny + 2, 2))),
            (gx < gx_n - 1, along_x(gx + 1), (pl.ds(nx, 2), mid_y), (pl.ds(0, 2), mid_y)),
            (gx > 0, along_x(gx - 1), (pl.ds(2, 2), mid_y), (pl.ds(nx + 2, 2), mid_y)),
        )
        return [
            (
                there,
                pltpu.make_async_remote_copy(
                    src_ref=wide.at[p, src[0], src[1]],
                    dst_ref=wide.at[p, dst[0], dst[1]],
                    send_sem=send_halo.at[p, way],
                    recv_sem=recv_halo.at[p, way],
                    device_id=who,
                    device_id_type=MESH,
                ),
            )
            for way, (there, who, src, dst) in enumerate(table)
        ]

    def visc_copies():
        table = (
            (gy < gy_n - 1, along_y(gy + 1)),
            (gy > 0, along_y(gy - 1)),
            (gx < gx_n - 1, along_x(gx + 1)),
            (gx > 0, along_x(gx - 1)),
        )
        return [
            (
                there,
                pltpu.make_async_remote_copy(
                    src_ref=visc_ref,
                    dst_ref=near_visc.at[way],
                    send_sem=send_visc.at[way],
                    recv_sem=recv_visc.at[way],
                    device_id=who,
                    device_id_type=MESH,
                ),
            )
            for way, (there, who) in enumerate(table)
        ]

    arrives = (gy > 0, gy < gy_n - 1, gx > 0, gx < gx_n - 1)
    arrives_direct = (from_below, from_above) + arrives[2:]

    def start(copies):
        for there, copy in copies:
            pl.when(there)(copy.start)

    def wait_recv(copies, comes):
        for way, (_, copy) in enumerate(copies):
            pl.when(comes[way])(copy.wait_recv)

    def wait_send(copies):
        for there, copy in copies:
            pl.when(there)(copy.wait_send)

    load(0).wait()
    spread(0)
    load_visc.wait()
    pl.semaphore_wait(barrier, gx_n + gy_n - 2)

    start(visc_copies())
    start_first(0)
    for p in range(1, chunks):
        load(p).wait()
        spread(p)
        if p < 3:
            start(halo_copies(p - 1))
            start_first(p)
    load_vel.wait()

    def border(way):
        rows_y = jnp.zeros((chunks, nx, 2, chunk, nz), jnp.float32)
        rows_x = jnp.zeros((chunks, 2, ny, chunk, nz), jnp.float32)
        if way == 0:
            wide[:, 2:nx + 2, 0:2] = rows_y
        elif way == 1:
            wide[:, 2:nx + 2, ny + 2:ny + 4] = rows_y
        elif way == 2:
            wide[:, 0:2, 2:ny + 2] = rows_x
        else:
            wide[:, nx + 2:nx + 4, 2:ny + 2] = rows_x

    for way in range(4):
        pl.when(jnp.logical_not(arrives[way]))(functools.partial(border, way))

    inv[...] = jnp.zeros_like(inv)
    pad_visc[...] = jnp.zeros_like(pad_visc)
    pad_visc[1:nx + 1, 1:ny + 1, :] = visc_ref[...]
    pass_on(0, False)
    pass_on(0, True)
    wait_recv(visc_copies(), arrives)

    def visc_border(way):
        if way == 0:
            pad_visc[1:nx + 1, 0:1, :] = near_visc[0, :, ny - 1:ny, :]
        elif way == 1:
            pad_visc[1:nx + 1, ny + 1:ny + 2, :] = near_visc[1, :, 0:1, :]
        elif way == 2:
            pad_visc[0:1, 1:ny + 1, :] = near_visc[2, nx - 1:nx, :, :]
        else:
            pad_visc[nx + 1:nx + 2, 1:ny + 1, :] = near_visc[3, 0:1, :, :]

    for way in range(4):
        pl.when(arrives[way])(functools.partial(visc_border, way))

    lane3 = lax.broadcasted_iota(jnp.int32, (nx, ny, nz), 2)
    mid = pad_visc[1:nx + 1, 1:ny + 1, :]
    around = (
        (pad_visc[2:nx + 2, 1:ny + 1, :], pad_visc[0:nx, 1:ny + 1, :]),
        (pad_visc[1:nx + 1, 2:ny + 2, :], pad_visc[1:nx + 1, 0:ny, :]),
        (
            jnp.where(lane3 < nz - 1, pltpu.roll(mid, nz - 1, 2), 0.0),
            jnp.where(lane3 > 0, pltpu.roll(mid, 1, 2), 0.0),
        ),
    )
    for d in range(3):
        coef[d, 0] = vel_ref[d] * (8.0 / 12.0)
        coef[d, 1] = vel_ref[d] * (1.0 / 12.0)
        coef[d, 2] = 0.5 * (mid + around[d][0])
        coef[d, 3] = 0.5 * (mid + around[d][1])

    lane = lax.broadcasted_iota(jnp.int32, (chunk, nz), 1)

    def stencil(p):
        def plane(i, carry):
            for j in range(ny):
                c = wide[p, i + 2, j + 2]
                near = (
                    (wide[p, i + 3, j + 2], wide[p, i + 1, j + 2], wide[p, i + 4, j + 2], wide[p, i, j + 2]),
                    (wide[p, i + 2, j + 3], wide[p, i + 2, j + 1], wide[p, i + 2, j + 4], wide[p, i + 2, j]),
                    (
                        jnp.where(lane < nz - 1, pltpu.roll(c, nz - 1, 1), 0.0),
                        jnp.where(lane > 0, pltpu.roll(c, 1, 1), 0.0),
                        jnp.where(lane < nz - 2, pltpu.roll(c, nz - 2, 1), 0.0),
                        jnp.where(lane > 1, pltpu.roll(c, 2, 1), 0.0),
                    ),
                )
                total = None
                for d in range(3):
                    up, down, up2, down2 = near[d]
                    w8, w1, vp, vm = (coef[d, t, i, pl.ds(j, 1), :] for t in range(4))
                    term = (w8 * (up - down) - w1 * (up2 - down2)) - (vp * (up - c) - vm * (c - down))
                    total = term if total is None else total + term
                lanes = pl.ds(pl.multiple_of((i * ny + j) * nz, nz), nz)
                upper = total.astype(jnp.bfloat16)
                high[pl.ds(p * chunk, chunk), lanes] = upper
                rest[pl.ds(p * chunk, chunk), lanes] = (total - upper.astype(jnp.float32)).astype(jnp.bfloat16)
            return carry

        lax.fori_loop(0, nx, plane, 0)

    def sum_copies(p, axis):
        me, count, who, part, send, recv = (
            (gy, gy_n, along_y, part_y, send_y, recv_y) if axis == "gy" else (gx, gx_n, along_x, part_x, send_x, recv_x)
        )
        out, into = [], []
        for off in range(1, count):
            to, frm = lax.rem(me + off, count), lax.rem(me + count - off, count)
            for list_, slot, k in ((out, me, to), (into, frm, frm)):
                list_.append(
                    pltpu.make_async_remote_copy(
                        src_ref=part.at[p, slot], dst_ref=part.at[p, slot],
                        send_sem=send.at[p, off], recv_sem=recv.at[p, off],
                        device_id=who(k), device_id_type=MESH,
                    )
                )
        return out, into

    def added(part, p, count):
        total = part[p, 0]
        for k in range(1, count):
            total = total + part[p, k]
        return total

    def halves_sum(with_high, with_rest):
        return with_high[:chunk] + (with_high[chunk:] + (with_rest[:chunk] + with_rest[chunk:]))

    def gram(p):
        top = (p + 1) * chunk
        both = jnp.concatenate([high[p * chunk:top, :], rest[p * chunk:top, :]], axis=0)
        panel = halves_sum(narrow_dot(both, high[0:top, :], True), narrow_dot(both, rest[0:top, :], True))
        panel = panel * (1.0 / cells_total)
        if top < snaps:
            panel = jnp.concatenate([panel, jnp.zeros((chunk, snaps - top), jnp.float32)], axis=1)
        part_y[p, gy] = panel
        for copy in sum_copies(p, "gy")[0]:
            copy.start()

    def gram_x(p):
        for copy in sum_copies(p, "gy")[1]:
            copy.wait_recv()
        part_x[p, gx] = added(part_y, p, gy_n)
        for copy in sum_copies(p, "gx")[0]:
            copy.start()

    row_s = lax.broadcasted_iota(jnp.int32, (chunk, snaps), 0)
    lane_s = lax.broadcasted_iota(jnp.int32, (chunk, snaps), 1)

    def padded(x):
        return x if chunk == snaps else jnp.concatenate([x, jnp.zeros((snaps - chunk, snaps), jnp.float32)], axis=0)

    def factor(p):
        for copy in sum_copies(p, "gx")[1]:
            copy.wait_recv()
        g = added(part_x, p, gx_n)
        w0 = p * chunk
        here = pl.ds(w0, chunk)
        if p > 0:
            off = dot(g, inv[...], transposed=True)
            g = pltpu.roll(g, snaps - w0, 1) - dot(off, padded(off), transposed=True)
            back = dot(off, inv[...])
            low[here, :] = off
        else:
            low[here, :] = jnp.zeros((chunk, snaps), jnp.float32)
        a = jnp.where(lane_s < chunk, g, jnp.where(lane_s == row_s + chunk, 1.0, 0.0))
        step = 8
        a = a.reshape(chunk // step, step, snaps)
        row_8 = lax.broadcasted_iota(jnp.int32, (step, snaps), 0)

        def splat(x, row):
            return jnp.broadcast_to(x[row:row + 1, :], (step, snaps))

        done = []
        for block in range(chunk // step):
            first = block * step
            own_rows, later = a[0], a[1:]
            columns = [jnp.broadcast_to(later[:, :, first + t:first + t + 1], later.shape) for t in range(step)]
            own_cols = [jnp.broadcast_to(own_rows[:, first + t:first + t + 1], (step, snaps)) for t in range(step)]
            entries = {(t, u): splat(own_cols[t], u) for t in range(step) for u in range(t, step)}
            rows = [splat(own_rows, t) for t in range(step)]
            for t in range(step):
                over = 1.0 / entries[t, t]
                scaled = rows[t] * over
                if later.shape[0]:
                    later = later - columns[t] * scaled[None]
                for u in range(t + 1, step):
                    ratio = entries[t, u] * over
                    for v in range(u, step):
                        entries[u, v] = entries[u, v] - ratio * entries[t, v]
                    rows[u] = rows[u] - ratio * rows[t]
                    if later.shape[0]:
                        columns[u] = columns[u] - columns[t] * ratio[None]
            kept = rows[0]
            for t in range(1, step):
                kept = jnp.where(row_8 == t, rows[t], kept)
            done.append(kept)
            a = later
        a = jnp.concatenate(done, axis=0)
        pivots = jnp.sum(jnp.where(lane_s == row_s, a, 0.0), axis=1, keepdims=True)
        a = a / jnp.sqrt(pivots)
        upper = jnp.where((lane_s >= row_s) & (lane_s < chunk), a, 0.0)
        own = jnp.where(lane_s < chunk, pltpu.roll(a, snaps - chunk, 1), 0.0)
        if p > 0:
            diag[here, :] = pltpu.roll(upper, w0, 1)
            inv[here, :] = pltpu.roll(own, w0, 1) - dot(own, padded(back))
        else:
            diag[here, :] = upper
            inv[here, :] = own

    def modes(p):
        top = (p + 1) * chunk
        full = inv[p * chunk:top, 0:top]
        upper = full.astype(jnp.bfloat16)
        weights = jnp.concatenate([upper, (full - upper.astype(jnp.float32)).astype(jnp.bfloat16)], axis=0)

        def plane(i, carry):
            first = pl.multiple_of(i * ny * nz, ny * nz)
            lanes = pl.ds(first, ny * nz)
            block = halves_sum(narrow_dot(weights, high[0:top, lanes]), narrow_dot(weights, rest[0:top, lanes]))
            for j in range(ny):
                rows_out[pl.ds(i * ny + j, chunk, stride=cells), :] = block[:, j * nz:(j + 1) * nz]
            return carry

        lax.fori_loop(0, nx, plane, 0)
        modes_ref[p * chunk * cells:top * cells, :] = rows_out[...].astype(jnp.bfloat16)

    for p in range(chunks):
        if p == 0:
            pass_on(1, False)
            pass_on(1, True)
        wait_send(halo_copies(p))
        if p + 2 < chunks:
            start(halo_copies(p + 2))
        if p + 3 < chunks:
            start_first(p + 3)
        if p + 2 < chunks:
            pass_on(p + 2, False)
            pass_on(p + 2, True)
        wait_recv(halo_copies(p), arrives_direct)
        wait_mid(p)
        stencil(p)
        gram(p)
        if p > 0:
            factor(p - 1)
        gram_x(p)
        if p > 0:
            modes(p - 1)
    factor(chunks - 1)
    modes(chunks - 1)
    factor_ref[...] = low[...].T + diag[...]

    wait_send(visc_copies())
    for p in range(chunks):
        wait_mid_sent(p)
        wait_passed(p)
        for axis in ("gy", "gx"):
            for copy in sum_copies(p, axis)[0]:
                copy.wait_send()


def per_device(gx_n, gy_n, snapshots, viscosity, velocity):
    snaps, nx, ny, nz = snapshots.shape
    cells = nx * ny
    chunk = snaps // 8
    chunks = snaps // chunk
    f32 = jnp.float32
    dma = pltpu.SemaphoreType.DMA
    vmem = pl.BlockSpec(memory_space=pltpu.VMEM)
    modes, factor = pl.pallas_call(
        functools.partial(
            kernel, (snaps, nx, ny, nz), (gx_n, gy_n), chunk, float(cells * nz * gx_n * gy_n)
        ),
        out_shape=(
            jax.ShapeDtypeStruct((snaps * cells, nz), jnp.bfloat16),
            jax.ShapeDtypeStruct((snaps, snaps), f32),
        ),
        in_specs=[pl.BlockSpec(memory_space=pltpu.HBM)] * 3,
        out_specs=(vmem, vmem),
        scratch_shapes=[
            pltpu.VMEM((snaps * cells, nz), f32),
            pltpu.VMEM((nx, ny, nz), f32),
            pltpu.VMEM((3, nx, ny, nz), f32),
            dma((chunks,)), dma((2,)),
            pltpu.VMEM((chunks, nx + 4, ny + 4, chunk, nz), f32),
            pltpu.VMEM((chunks, 2, nx // 2, 2, chunk, nz), f32),
            pltpu.VMEM((4, nx, ny, nz), f32),
            pltpu.VMEM((nx + 2, ny + 2, nz), f32),
            pltpu.VMEM((3, 4, nx, ny, nz), f32),
            pltpu.VMEM((snaps, cells * nz), jnp.bfloat16),
            pltpu.VMEM((snaps, cells * nz), jnp.bfloat16),
            pltpu.VMEM((chunk * cells, nz), f32),
            pltpu.VMEM((chunks, gy_n, chunk, snaps), f32),
            pltpu.VMEM((chunks, gx_n, chunk, snaps), f32),
            pltpu.VMEM((snaps, snaps), f32),
            pltpu.VMEM((snaps, snaps), f32),
            pltpu.VMEM((snaps, snaps), f32),
            dma((chunks, 4)), dma((chunks, 4)), dma((chunks, 2)), dma((chunks, 2)), dma((chunks, 2)), dma((chunks, 2)),
            dma((4,)), dma((4,)),
            dma((chunks, gy_n)), dma((chunks, gy_n)), dma((chunks, gx_n)), dma((chunks, gx_n)),
        ],
        compiler_params=pltpu.CompilerParams(
            collective_id=0, has_side_effects=True, vmem_limit_bytes=51 * 1024 * 1024
        ),
        name="pod",
    )(snapshots.reshape(snaps * cells, nz), viscosity, velocity)
    return modes.reshape(snaps, nx, ny, nz), factor


def solution(mesh):
    placed = (P(None, "gx", "gy", None), P("gx", "gy", None), P(None, "gx", "gy", None))
    return jax.shard_map(
        functools.partial(per_device, mesh.shape["gx"], mesh.shape["gy"]),
        mesh=mesh,
        in_specs=placed,
        out_specs=(P(None, "gx", "gy", None), P()),
        check_vma=False,
    )
```

```python
import functools

import jax
import jax.numpy as jnp
from jax import lax
from jax.experimental import pallas as pl
from jax.experimental.pallas import tpu as pltpu
from jax.sharding import PartitionSpec as P

MESH = pl.DeviceIdType.MESH
HIGH = lax.Precision.HIGHEST


def dot(a, b, transposed=False):
    return lax.dot_general(
        a, b, (((1,), (1 if transposed else 0,)), ((), ())),
        precision=HIGH, preferred_element_type=jnp.float32,
    )


def narrow_dot(a, b, transposed=False):
    return lax.dot_general(
        a, b, (((1,), (1 if transposed else 0,)), ((), ())), preferred_element_type=jnp.float32
    )


def kernel(
    dims, peers, chunk, cells_total,
    snap_any, visc_any, vel_any, modes_ref, factor_ref,
    snap_ref, visc_ref, vel_ref, load_snap, load_rest, wide, passing, near_visc, pad_visc, coef, high, rest, rows_out, part_y, part_x, inv, low, diag,
    send_halo, recv_halo, send_mid, recv_pass, send_pass, recv_mid, send_visc, recv_visc, send_y, recv_y, send_x, recv_x,
):
    snaps, nx, ny, nz = dims
    gx_n, gy_n = peers
    cells = nx * ny
    chunks = snaps // chunk
    gx, gy = lax.axis_index("gx"), lax.axis_index("gy")

    def along_y(other):
        return {"gx": gx, "gy": other}

    def along_x(other):
        return {"gx": other, "gy": gy}

    def load(p):
        here = pl.ds(p * chunk * cells, chunk * cells)
        return pltpu.make_async_copy(snap_any.at[here], snap_ref.at[here], load_snap.at[p])

    load_visc = pltpu.make_async_copy(visc_any, visc_ref, load_rest.at[0])
    load_vel = pltpu.make_async_copy(vel_any, vel_ref, load_rest.at[1])
    load(0).start()
    load_visc.start()
    for p in range(1, chunks):
        load(p).start()
    load_vel.start()

    barrier = pltpu.get_barrier_semaphore()
    for off in range(1, gy_n):
        pl.semaphore_signal(barrier, inc=1, device_id=along_y(lax.rem(gy + off, gy_n)), device_id_type=MESH)
    for off in range(1, gx_n):
        pl.semaphore_signal(barrier, inc=1, device_id=along_x(lax.rem(gx + off, gx_n)), device_id_type=MESH)

    def spread(p):
        def plane(i, carry):
            for j in range(ny):
                wide[p, i + 2, j + 2] = snap_ref[
                    pl.ds(p * chunk * cells + i * ny + j, chunk, stride=cells), :
                ]
            return carry

        lax.fori_loop(0, nx, plane, 0)

    relayed = gy_n == 4
    if relayed:
        up_direct, down_direct = (gy == 0) | (gy == 2), (gy == 1) | (gy == 3)
        from_below, from_above = down_direct, up_direct
    else:
        up_direct, down_direct = gy < gy_n - 1, gy > 0
        from_below, from_above = gy > 0, gy < gy_n - 1
    half = nx // 2
    halves = (pl.ds(2, half), pl.ds(2 + half, half))
    mids = ((1, ny, 0, 0, (0, 3)), (2, 2, ny + 2, 1, (3, 0)))

    def first_hop(p, slot, h):
        _, row, _, _, relays = mids[slot]
        return pltpu.make_async_remote_copy(
            src_ref=wide.at[p, halves[h], pl.ds(row, 2)], dst_ref=passing.at[p, slot],
            send_sem=send_mid.at[p, int(h)], recv_sem=recv_pass.at[p, slot],
            device_id=along_y(relays[h]), device_id_type=MESH,
        )

    def first_hops(p, me):
        return [first_hop(p, me - 1, h) for h in (1, 0)]

    def second_hop(p, slot, relay):
        source, _, row, _, relays = mids[slot]
        h = relays.index(relay)
        return pltpu.make_async_remote_copy(
            src_ref=passing.at[p, slot], dst_ref=wide.at[p, halves[h], pl.ds(row, 2)],
            send_sem=send_pass.at[p, slot], recv_sem=recv_mid.at[p, h],
            device_id=along_y(3 - source), device_id_type=MESH,
        )

    def when_at(me, body):
        pl.when(gy == me)(body)

    def start_first(p):
        if relayed:
            for me in (1, 2):
                def go(me=me):
                    for copy in first_hops(p, me):
                        copy.start()
                when_at(me, go)

    def pass_on(p, late):
        if relayed:
            for relay in (0, 3):
                def go(relay=relay):
                    slot = (relay == 3) ^ (not late)
                    copy = second_hop(p, int(slot), relay)
                    first_hop(p, int(slot), mids[slot][4].index(relay)).wait_recv()
                    copy.start()
                when_at(relay, go)

    def wait_mid(p):
        if relayed:
            for me in (1, 2):
                def go(me=me):
                    for relay in mids[2 - me][4]:
                        second_hop(p, 2 - me, relay).wait_recv()
                when_at(me, go)

    def wait_mid_sent(p):
        if relayed:
            for me in (1, 2):
                def go(me=me):
                    for copy in first_hops(p, me):
                        copy.wait_send()
                when_at(me, go)

    def wait_passed(p):
        if relayed:
            for relay in (0, 3):
                def go(relay=relay):
                    for slot in range(2):
                        second_hop(p, slot, relay).wait_send()
                when_at(relay, go)

    def halo_copies(p):
        mid_x, mid_y = pl.ds(2, nx), pl.ds(2, ny)
        table = (
            (up_direct, along_y(gy + 1), (mid_x, pl.ds(ny, 2)), (mid_x, pl.ds(0, 2))),
            (down_direct, along_y(gy - 1), (mid_x, pl.ds(2, 2)), (mid_x, pl.ds(ny + 2, 2))),
            (gx < gx_n - 1, along_x(gx + 1), (pl.ds(nx, 2), mid_y), (pl.ds(0, 2), mid_y)),
            (gx > 0, along_x(gx - 1), (pl.ds(2, 2), mid_y), (pl.ds(nx + 2, 2), mid_y)),
        )
        return [
            (
                there,
                pltpu.make_async_remote_copy(
                    src_ref=wide.at[p, src[0], src[1]],
                    dst_ref=wide.at[p, dst[0], dst[1]],
                    send_sem=send_halo.at[p, way],
                    recv_sem=recv_halo.at[p, way],
                    device_id=who,
                    device_id_type=MESH,
                ),
            )
            for way, (there, who, src, dst) in enumerate(table)
        ]

    def visc_copies():
        table = (
            (gy < gy_n - 1, along_y(gy + 1)),
            (gy > 0, along_y(gy - 1)),
            (gx < gx_n - 1, along_x(gx + 1)),
            (gx > 0, along_x(gx - 1)),
        )
        return [
            (
                there,
                pltpu.make_async_remote_copy(
                    src_ref=visc_ref,
                    dst_ref=near_visc.at[way],
                    send_sem=send_visc.at[way],
                    recv_sem=recv_visc.at[way],
                    device_id=who,
                    device_id_type=MESH,
                ),
            )
            for way, (there, who) in enumerate(table)
        ]

    arrives = (gy > 0, gy < gy_n - 1, gx > 0, gx < gx_n - 1)
    arrives_direct = (from_below, from_above) + arrives[2:]

    def start(copies):
        for there, copy in copies:
            pl.when(there)(copy.start)

    def wait_recv(copies, comes):
        for way, (_, copy) in enumerate(copies):
            pl.when(comes[way])(copy.wait_recv)

    def wait_send(copies):
        for there, copy in copies:
            pl.when(there)(copy.wait_send)

    load(0).wait()
    spread(0)
    load_visc.wait()
    pl.semaphore_wait(barrier, gx_n + gy_n - 2)

    start(visc_copies())
    start_first(0)
    start(halo_copies(0))
    for p in range(1, chunks):
        load(p).wait()
        spread(p)
        if p == 1:
            start_first(1)
    load_vel.wait()

    def border(way):
        rows_y = jnp.zeros((chunks, nx, 2, chunk, nz), jnp.float32)
        rows_x = jnp.zeros((chunks, 2, ny, chunk, nz), jnp.float32)
        if way == 0:
            wide[:, 2:nx + 2, 0:2] = rows_y
        elif way == 1:
            wide[:, 2:nx + 2, ny + 2:ny + 4] = rows_y
        elif way == 2:
            wide[:, 0:2, 2:ny + 2] = rows_x
        else:
            wide[:, nx + 2:nx + 4, 2:ny + 2] = rows_x

    for way in range(4):
        pl.when(jnp.logical_not(arrives[way]))(functools.partial(border, way))

    inv[...] = jnp.zeros_like(inv)
    pad_visc[...] = jnp.zeros_like(pad_visc)
    pad_visc[1:nx + 1, 1:ny + 1, :] = visc_ref[...]
    pass_on(0, False)
    pass_on(0, True)
    wait_recv(visc_copies(), arrives)

    def visc_border(way):
        if way == 0:
            pad_visc[1:nx + 1, 0:1, :] = near_visc[0, :, ny - 1:ny, :]
        elif way == 1:
            pad_visc[1:nx + 1, ny + 1:ny + 2, :] = near_visc[1, :, 0:1, :]
        elif way == 2:
            pad_visc[0:1, 1:ny + 1, :] = near_visc[2, nx - 1:nx, :, :]
        else:
            pad_visc[nx + 1:nx + 2, 1:ny + 1, :] = near_visc[3, 0:1, :, :]

    for way in range(4):
        pl.when(arrives[way])(functools.partial(visc_border, way))

    lane3 = lax.broadcasted_iota(jnp.int32, (nx, ny, nz), 2)
    mid = pad_visc[1:nx + 1, 1:ny + 1, :]
    around = (
        (pad_visc[2:nx + 2, 1:ny + 1, :], pad_visc[0:nx, 1:ny + 1, :]),
        (pad_visc[1:nx + 1, 2:ny + 2, :], pad_visc[1:nx + 1, 0:ny, :]),
        (
            jnp.where(lane3 < nz - 1, pltpu.roll(mid, nz - 1, 2), 0.0),
            jnp.where(lane3 > 0, pltpu.roll(mid, 1, 2), 0.0),
        ),
    )
    for d in range(3):
        coef[d, 0] = vel_ref[d] * (8.0 / 12.0)
        coef[d, 1] = vel_ref[d] * (1.0 / 12.0)
        coef[d, 2] = 0.5 * (mid + around[d][0])
        coef[d, 3] = 0.5 * (mid + around[d][1])

    lane = lax.broadcasted_iota(jnp.int32, (chunk, nz), 1)

    def stencil(p):
        def plane(i, carry):
            for j in range(ny):
                c = wide[p, i + 2, j + 2]
                near = (
                    (wide[p, i + 3, j + 2], wide[p, i + 1, j + 2], wide[p, i + 4, j + 2], wide[p, i, j + 2]),
                    (wide[p, i + 2, j + 3], wide[p, i + 2, j + 1], wide[p, i + 2, j + 4], wide[p, i + 2, j]),
                    (
                        jnp.where(lane < nz - 1, pltpu.roll(c, nz - 1, 1), 0.0),
                        jnp.where(lane > 0, pltpu.roll(c, 1, 1), 0.0),
                        jnp.where(lane < nz - 2, pltpu.roll(c, nz - 2, 1), 0.0),
                        jnp.where(lane > 1, pltpu.roll(c, 2, 1), 0.0),
                    ),
                )
                total = None
                for d in range(3):
                    up, down, up2, down2 = near[d]
                    w8, w1, vp, vm = (coef[d, t, i, pl.ds(j, 1), :] for t in range(4))
                    term = (w8 * (up - down) - w1 * (up2 - down2)) - (vp * (up - c) - vm * (c - down))
                    total = term if total is None else total + term
                lanes = pl.ds(pl.multiple_of((i * ny + j) * nz, nz), nz)
                upper = total.astype(jnp.bfloat16)
                high[pl.ds(p * chunk, chunk), lanes] = upper
                rest[pl.ds(p * chunk, chunk), lanes] = (total - upper.astype(jnp.float32)).astype(jnp.bfloat16)
            return carry

        lax.fori_loop(0, nx, plane, 0)

    def sum_copies(p, axis):
        me, count, who, part, send, recv = (
            (gy, gy_n, along_y, part_y, send_y, recv_y) if axis == "gy" else (gx, gx_n, along_x, part_x, send_x, recv_x)
        )
        out, into = [], []
        for off in range(1, count):
            to, frm = lax.rem(me + off, count), lax.rem(me + count - off, count)
            for list_, slot, k in ((out, me, to), (into, frm, frm)):
                list_.append(
                    pltpu.make_async_remote_copy(
                        src_ref=part.at[p, slot], dst_ref=part.at[p, slot],
                        send_sem=send.at[p, off], recv_sem=recv.at[p, off],
                        device_id=who(k), device_id_type=MESH,
                    )
                )
        return out, into

    def added(part, p, count):
        total = part[p, 0]
        for k in range(1, count):
            total = total + part[p, k]
        return total

    def halves_sum(with_high, with_rest):
        return with_high[:chunk] + (with_high[chunk:] + (with_rest[:chunk] + with_rest[chunk:]))

    def gram(p):
        top = (p + 1) * chunk
        both = jnp.concatenate([high[p * chunk:top, :], rest[p * chunk:top, :]], axis=0)
        panel = halves_sum(narrow_dot(both, high[0:top, :], True), narrow_dot(both, rest[0:top, :], True))
        panel = panel * (1.0 / cells_total)
        if top < snaps:
            panel = jnp.concatenate([panel, jnp.zeros((chunk, snaps - top), jnp.float32)], axis=1)
        part_y[p, gy] = panel
        for copy in sum_copies(p, "gy")[0]:
            copy.start()

    def gram_x(p):
        for copy in sum_copies(p, "gy")[1]:
            copy.wait_recv()
        part_x[p, gx] = added(part_y, p, gy_n)
        for copy in sum_copies(p, "gx")[0]:
            copy.start()

    row_s = lax.broadcasted_iota(jnp.int32, (chunk, snaps), 0)
    lane_s = lax.broadcasted_iota(jnp.int32, (chunk, snaps), 1)

    def padded(x):
        return x if chunk == snaps else jnp.concatenate([x, jnp.zeros((snaps - chunk, snaps), jnp.float32)], axis=0)

    def factor(p):
        for copy in sum_copies(p, "gx")[1]:
            copy.wait_recv()
        g = added(part_x, p, gx_n)
        w0 = p * chunk
        here = pl.ds(w0, chunk)
        if p > 0:
            off = dot(g, inv[...], transposed=True)
            g = pltpu.roll(g, snaps - w0, 1) - dot(off, padded(off), transposed=True)
            back = dot(off, inv[...])
            low[here, :] = off
        else:
            low[here, :] = jnp.zeros((chunk, snaps), jnp.float32)
        a = jnp.where(lane_s < chunk, g, jnp.where(lane_s == row_s + chunk, 1.0, 0.0))
        step = 8
        a = a.reshape(chunk // step, step, snaps)
        row_8 = lax.broadcasted_iota(jnp.int32, (step, snaps), 0)

        def splat(x, row):
            return jnp.broadcast_to(x[row:row + 1, :], (step, snaps))

        done = []
        for block in range(chunk // step):
            first = block * step
            own_rows, later = a[0], a[1:]
            columns = [jnp.broadcast_to(later[:, :, first + t:first + t + 1], later.shape) for t in range(step)]
            own_cols = [jnp.broadcast_to(own_rows[:, first + t:first + t + 1], (step, snaps)) for t in range(step)]
            entries = {(t, u): splat(own_cols[t], u) for t in range(step) for u in range(t, step)}
            rows = [splat(own_rows, t) for t in range(step)]
            for t in range(step):
                over = 1.0 / entries[t, t]
                scaled = rows[t] * over
                if later.shape[0]:
                    later = later - columns[t] * scaled[None]
                for u in range(t + 1, step):
                    ratio = entries[t, u] * over
                    for v in range(u, step):
                        entries[u, v] = entries[u, v] - ratio * entries[t, v]
                    rows[u] = rows[u] - ratio * rows[t]
                    if later.shape[0]:
                        columns[u] = columns[u] - columns[t] * ratio[None]
            kept = rows[0]
            for t in range(1, step):
                kept = jnp.where(row_8 == t, rows[t], kept)
            done.append(kept)
            a = later
        a = jnp.concatenate(done, axis=0)
        pivots = jnp.sum(jnp.where(lane_s == row_s, a, 0.0), axis=1, keepdims=True)
        a = a / jnp.sqrt(pivots)
        upper = jnp.where((lane_s >= row_s) & (lane_s < chunk), a, 0.0)
        own = jnp.where(lane_s < chunk, pltpu.roll(a, snaps - chunk, 1), 0.0)
        if p > 0:
            diag[here, :] = pltpu.roll(upper, w0, 1)
            inv[here, :] = pltpu.roll(own, w0, 1) - dot(own, padded(back))
        else:
            diag[here, :] = upper
            inv[here, :] = own

    def modes(p):
        top = (p + 1) * chunk
        full = inv[p * chunk:top, 0:top]
        upper = full.astype(jnp.bfloat16)
        weights = jnp.concatenate([upper, (full - upper.astype(jnp.float32)).astype(jnp.bfloat16)], axis=0)

        def plane(i, carry):
            first = pl.multiple_of(i * ny * nz, ny * nz)
            lanes = pl.ds(first, ny * nz)
            block = halves_sum(narrow_dot(weights, high[0:top, lanes]), narrow_dot(weights, rest[0:top, lanes]))
            for j in range(ny):
                rows_out[pl.ds(i * ny + j, chunk, stride=cells), :] = block[:, j * nz:(j + 1) * nz]
            return carry

        lax.fori_loop(0, nx, plane, 0)
        modes_ref[p * chunk * cells:top * cells, :] = rows_out[...].astype(jnp.bfloat16)

    for p in range(chunks):
        wait_send(halo_copies(p))
        if p + 1 < chunks:
            start(halo_copies(p + 1))
        if p + 2 < chunks:
            start_first(p + 2)
        if p + 1 < chunks:
            pass_on(p + 1, False)
            pass_on(p + 1, True)
        wait_recv(halo_copies(p), arrives_direct)
        wait_mid(p)
        stencil(p)
        gram(p)
        gram_x(p)
        factor(p)
        modes(p)
    factor_ref[...] = low[...].T + diag[...]

    wait_send(visc_copies())
    for p in range(chunks):
        wait_mid_sent(p)
        wait_passed(p)
        for axis in ("gy", "gx"):
            for copy in sum_copies(p, axis)[0]:
                copy.wait_send()


def per_device(gx_n, gy_n, snapshots, viscosity, velocity):
    snaps, nx, ny, nz = snapshots.shape
    cells = nx * ny
    chunk = snaps // 2
    chunks = snaps // chunk
    f32 = jnp.float32
    dma = pltpu.SemaphoreType.DMA
    vmem = pl.BlockSpec(memory_space=pltpu.VMEM)
    modes, factor = pl.pallas_call(
        functools.partial(
            kernel, (snaps, nx, ny, nz), (gx_n, gy_n), chunk, float(cells * nz * gx_n * gy_n)
        ),
        out_shape=(
            jax.ShapeDtypeStruct((snaps * cells, nz), jnp.bfloat16),
            jax.ShapeDtypeStruct((snaps, snaps), f32),
        ),
        in_specs=[pl.BlockSpec(memory_space=pltpu.HBM)] * 3,
        out_specs=(vmem, vmem),
        scratch_shapes=[
            pltpu.VMEM((snaps * cells, nz), f32),
            pltpu.VMEM((nx, ny, nz), f32),
            pltpu.VMEM((3, nx, ny, nz), f32),
            dma((chunks,)), dma((2,)),
            pltpu.VMEM((chunks, nx + 4, ny + 4, chunk, nz), f32),
            pltpu.VMEM((chunks, 2, nx // 2, 2, chunk, nz), f32),
            pltpu.VMEM((4, nx, ny, nz), f32),
            pltpu.VMEM((nx + 2, ny + 2, nz), f32),
            pltpu.VMEM((3, 4, nx, ny, nz), f32),
            pltpu.VMEM((snaps, cells * nz), jnp.bfloat16),
            pltpu.VMEM((snaps, cells * nz), jnp.bfloat16),
            pltpu.VMEM((chunk * cells, nz), f32),
            pltpu.VMEM((chunks, gy_n, chunk, snaps), f32),
            pltpu.VMEM((chunks, gx_n, chunk, snaps), f32),
            pltpu.VMEM((snaps, snaps), f32),
            pltpu.VMEM((snaps, snaps), f32),
            pltpu.VMEM((snaps, snaps), f32),
            dma((chunks, 4)), dma((chunks, 4)), dma((chunks, 2)), dma((chunks, 2)), dma((chunks, 2)), dma((chunks, 2)),
            dma((4,)), dma((4,)),
            dma((chunks, gy_n)), dma((chunks, gy_n)), dma((chunks, gx_n)), dma((chunks, gx_n)),
        ],
        compiler_params=pltpu.CompilerParams(
            collective_id=0, has_side_effects=True, vmem_limit_bytes=51 * 1024 * 1024
        ),
        name="pod",
    )(snapshots.reshape(snaps * cells, nz), viscosity, velocity)
    return modes.reshape(snaps, nx, ny, nz), factor


def solution(mesh):
    placed = (P(None, "gx", "gy", None), P("gx", "gy", None), P(None, "gx", "gy", None))
    return jax.shard_map(
        functools.partial(per_device, mesh.shape["gx"], mesh.shape["gy"]),
        mesh=mesh,
        in_specs=placed,
        out_specs=(P(None, "gx", "gy", None), P()),
        check_vma=False,
    )
```
